32 devices in a mesh: req: 4 (over z), seq: 8 (over y, x, core).
Axes of the slice: x: 2, y: 2, z: 4, core: 2. Of those that a mesh axis runs over, the one named last changes fastest.
Arguments:
- queries: bfloat16 [4, 128, 4096], P('req', 'seq'), may hold values from -160 to 160
- kv_cache: bfloat16 [4, 4096, 2, 256], P('req', 'seq'), may hold values from -6 to 6
- tree_kv: bfloat16 [4, 128, 2, 256], P('req', 'seq'), may hold values from -14 to 14
- context_lengths: int32 [4], P('req'), may hold values from 512 to 4096, as said below
- tree_parents: int32 [4, 128], P('req'), may hold values from -1 to 126, as said below
- resid: bfloat16 [4, 128, 4096], P('req', 'seq'), may hold values from -6 to 6
- out_weight: bfloat16 [4096, 4096], P('seq'), may hold values from -0.5 to 0.5
- norm_gain: bfloat16 [4096], replicated, may hold values from 0.099609375 to 1.8984375
- expert_ids: int32 [4, 128, 8], P('req'), may hold values from 0 to 63, all different within a row; in each aligned block of 128 rows (0 to 127, 128 to 255, ..., all dimensions but the last counted through in order) at most 32 rows name the same one
- gate_weights: bfloat16 [4, 128, 8], P('req'), may hold values from 0.049804688 to 0.5
- w_gate: bfloat16 [512, 4096, 128], P(('req', 'seq')), may hold values from -0.09375 to 0.09375
- w_up: bfloat16 [512, 4096, 128], P(('req', 'seq')), may hold values from -0.09375 to 0.09375
- w_down: bfloat16 [512, 128, 4096], P(('req', 'seq')), may hold values from -0.375 to 0.375
Outputs:
- attended: bfloat16 [4, 128, 4096], P('req', 'seq')
- expert_sum: bfloat16 [4, 128, 4096], P('req', 'seq')
The draws below stay inside these ranges and needn't reach their ends.
Inputs may be any that keep to these rules, and one draw needn't show every extreme that they name: `expert_ids`: each row names 8 different experts; among the rows of one request no expert is named by more than 32 rows. `tree_parents`: each request holds 4 trees of 32 nodes in a row; a tree's first node has parent -1, every other node's parent is an earlier node of the same tree; the request's last node has parent 128 - 2. `context_lengths`: at least one request uses all 4096 positions.
All inputs are finite; a program needn't handle non-finite values.
Results may differ from the reference program's by a relative error of at most 0.01615.
Values may be sent and summed in bfloat16 or wider, within the bound.
No kernel may reach another device: no remote copies, remote signals or barrier semaphores. Data moves between devices by JAX's collectives and lax.ppermute only.
A program may use at most 128 MiB of HBM per device.

```python
import math
import jax
import jax.numpy as jnp
import numpy as np
from jax import lax

D = 4096
DH = 128
HQ = 32
KVH = 2
EXPERTS = 64
FF_WIN = 1024
HID_DEV = 128
TOPK = 8
TREE = 32
CAP = 32
C_DEV = 512
ROWS = 128
SPLIT = 8
PANELS = 512
CTX = 4096
REQUESTS = 4
N_SEQ = 8


def cache_base(key):
    base = jax.random.normal(jax.random.fold_in(key, 11), (REQUESTS, CTX, 2, KVH * DH), jnp.float32)
    return jnp.clip(base, -6.0, 6.0)


def draw_kv_cache(key, part):
    base = cache_base(key)
    return base.astype(jnp.bfloat16)


def draw_queries(key, part):
    base = jax.random.normal(jax.random.fold_in(key, 12), (REQUESTS, ROWS, HQ * DH), jnp.float32)
    base = jnp.clip(base, -6.0, 6.0)
    return base.astype(jnp.bfloat16)


def draw_context_lengths(key, part):
    lengths = jax.random.randint(jax.random.fold_in(key, 21), (REQUESTS,), CTX // 8, CTX + 1)
    which = jax.random.randint(jax.random.fold_in(key, 22), (), 0, REQUESTS)
    return jnp.where(jnp.arange(REQUESTS) == which, CTX, lengths).astype(jnp.int32)


def draw_tree_parents(key, part):
    node = jnp.arange(ROWS, dtype=jnp.int32)
    local = node % TREE
    first = node - local
    raw = jax.random.randint(jax.random.fold_in(key, 31), (REQUESTS, ROWS), 0, 1048576)
    chosen = raw % jnp.maximum(local, 1)[None, :]
    parents = jnp.where(local[None, :] == 0, -1, first[None, :] + chosen)
    parents = jnp.where(node[None, :] == ROWS - 1, ROWS - 2, parents)
    return parents.astype(jnp.int32)


def steps_of(own_key, dims, split, low, largest):
    gain, own = 1.0, jax.random.fold_in(own_key, 6)
    for axis_at, parts in split:
        draws = jnp.exp(jax.random.uniform(jax.random.fold_in(own, axis_at), (parts,), jnp.float32, low / len(split), largest / len(split)))
        gain = gain * jnp.repeat(draws, dims[axis_at] // parts).reshape([-1 if axis == axis_at else 1 for axis in range(len(dims))])
    return gain


def shared_out(key, own, number, rows, count, top, bound, lean):
    sequence = jax.random.permutation(key, count)
    heavy_load, usual = load_shares(count, rows * top, bound, lean, True), load_shares(count, rows * top, bound, lean, False)
    places = jnp.arange(count)

    def named(sizes, rotation):
        used = int((sizes > 0).sum())
        fixed = max(1, used // 4)
        passed = fixed + (places - fixed + rotation * (used - fixed)) % max(1, count - fixed)
        return jnp.zeros((count,), jnp.int32).at[sequence[jnp.where(places < fixed, places, passed)]].set(jnp.asarray(sizes, jnp.int32))

    sizes = jnp.where(number % 4 == 0, named(heavy_load, number // 4), named(usual, number - number // 4 - 1))
    mixed = jax.random.permutation(jax.random.fold_in(own, 3), count)
    donor, sink = mixed[0:count // 2 * 2:2], mixed[1:count // 2 * 2:2]
    slack = jnp.minimum(sizes[donor] - 1, bound - sizes[sink]) // 2
    slack = jnp.where((donor == sequence[0]) | (sink == sequence[0]) | (sizes[sink] == 0), 0, jnp.maximum(slack, 0))
    passed = jax.random.randint(jax.random.fold_in(own, 4), (count // 2,), 0, 1 << 20) % (slack + 1)
    sizes = sizes.at[donor].add(-passed).at[sink].add(passed)
    items = jnp.searchsorted(jnp.cumsum(sizes), jnp.arange(rows * top), side="right").astype(jnp.int32)
    listing = items.reshape(top, rows).T
    listing = listing[jax.random.permutation(jax.random.fold_in(own, 1), rows)]
    rotation = jax.random.randint(jax.random.fold_in(own, 2), (rows, 1), 0, top)
    return jnp.take_along_axis(listing, (jnp.arange(top)[None, :] + rotation) % top, axis=1)


def load_shares(number_of, total, limit, lean, full):
    loads = [(1 << 20) // math.isqrt(rank ** lean) + 1 for rank in range(1, number_of + 1)]
    largest = limit if full else min(limit, max(-(-total // number_of), total * loads[0] // sum(loads)))
    least = 1 if total - largest >= number_of - 1 else 0
    counts, rest = [largest] + [least] * (number_of - 1), total - largest - least * (number_of - 1)
    while rest > 0:
        movable = [i for i in range(1, number_of) if counts[i] < largest] or [i for i in range(1, number_of) if counts[i] < limit]
        mass, left = sum([loads[i] for i in movable]), rest
        for i in movable:
            addition = min(limit - counts[i], max(1, left * loads[i] // mass), rest)
            counts[i] = counts[i] + addition
            rest = rest - addition
    return np.array(counts)


def scatter_about(own_key, dims, spread, bound, cuts=(), held_as=jnp.bfloat16):
    loudness = steps_of(own_key, dims, cuts, -0.22, 0.18) if cuts else 1.0
    values = jax.random.normal(own_key, dims, jnp.float32) * spread * loudness
    return jnp.minimum(jnp.maximum(values, -bound), bound).astype(held_as)


def setup_inputs(seed: int = 0) -> dict:
    seeds = jax.random.split(jax.random.key(seed), 14)
    queries = draw_queries(jax.random.fold_in(seeds[13], 71), 0)
    kv_cache = draw_kv_cache(jax.random.fold_in(seeds[13], 71), 0)
    tree_kv = scatter_about(seeds[2], (REQUESTS, ROWS, 2, KVH * DH), 3.5, 14.0, ((0, 4), (1, 8)))
    context_lengths = draw_context_lengths(jax.random.fold_in(seeds[13], 71), 0)
    tree_parents = draw_tree_parents(jax.random.fold_in(seeds[13], 71), 0)
    resid = scatter_about(seeds[5], (REQUESTS, ROWS, D), 1.0, 6.0, ((0, 4), (1, 8)))
    out_weight = scatter_about(seeds[6], (HQ * DH, D), 0.08, 0.5, ((0, 8),))
    norm_gain = jnp.clip(1.0 + 0.18 * jax.random.normal(seeds[7], (D,), jnp.float32), 0.099609375, 1.8984375).astype(jnp.bfloat16)
    expert_ids_keys = jax.random.split(jax.random.fold_in(seeds[8], 1), REQUESTS * ROWS // ROWS)
    expert_ids_turns = jax.random.permutation(jax.random.fold_in(seeds[8], 3), REQUESTS * ROWS // ROWS)
    expert_ids = jax.vmap(lambda own, number: shared_out(jax.random.fold_in(seeds[8], 2), own, number, ROWS, EXPERTS, TOPK, CAP, 1))(expert_ids_keys, expert_ids_turns).reshape((REQUESTS, ROWS, TOPK))
    gate_weights = jnp.clip(jnp.exp(math.log(0.5) - 2.306499 * jax.random.uniform(seeds[9], (REQUESTS, ROWS, TOPK), jnp.float32) ** steps_of(seeds[9], (REQUESTS, ROWS, TOPK), ((0, 4),), -0.2, 0.2)), 0.049804688, 0.5).astype(jnp.bfloat16)
    w_gate = scatter_about(seeds[10], (PANELS, D, HID_DEV), D ** -0.5, 0.09375, ((0, 32),))
    w_up = scatter_about(seeds[11], (PANELS, D, HID_DEV), D ** -0.5, 0.09375, ((0, 32),))
    w_down = scatter_about(seeds[12], (PANELS, HID_DEV, D), (FF_WIN // 4) ** -0.5, 0.375, ((0, 32),))
    return {"queries": queries, "kv_cache": kv_cache, "tree_kv": tree_kv, "context_lengths": context_lengths, "tree_parents": tree_parents, "resid": resid, "out_weight": out_weight, "norm_gain": norm_gain, "expert_ids": expert_ids, "gate_weights": gate_weights, "w_gate": w_gate, "w_up": w_up, "w_down": w_down}


NEG = -1e+30
EPS = 1e-06

def ancestry(parents):
    count = parents.shape[0]
    node = jnp.arange(count, dtype=jnp.int32)
    linked = (parents[:, None] == node[None, :]) | (node[:, None] == node[None, :])
    reach = linked.astype(jnp.float32)
    hops = 1
    while hops < count:
        reach = jnp.minimum(jnp.dot(reach, reach, preferred_element_type=jnp.float32), 1.0)
        hops = hops * 2
    return reach > 0.5

def rounded(value):
    return lax.optimization_barrier(value.astype(jnp.bfloat16)).astype(jnp.float32)

def attend(query, cache, tree, length, parents):
    group = HQ // KVH
    scale = DH ** (-0.5)
    heads = query.astype(jnp.float32).reshape(ROWS, KVH, group, DH)

    def shard(carry, index):
        block = lax.dynamic_slice_in_dim(cache, (index * C_DEV).astype(jnp.int32), C_DEV, 0).astype(jnp.float32)
        keys = block[:, 0].reshape(C_DEV, KVH, DH)
        values = block[:, 1].reshape(C_DEV, KVH, DH)
        scores = jnp.einsum('rkgd,tkd->rkgt', heads, keys) * scale
        valid = index * C_DEV + jnp.arange(C_DEV, dtype=jnp.int32) < length
        top = lax.optimization_barrier(jnp.max(jnp.where(valid, scores, NEG), axis=-1))
        weights = jnp.where(valid, jnp.exp(scores - top[..., None]), 0.0)
        total = lax.optimization_barrier(jnp.sum(weights, axis=-1))
        out = jnp.einsum('rkgt,tkd->rkgd', rounded(weights), values)
        return (carry, (top, total, out))
    _, (tops, totals, outs) = lax.scan(shard, jnp.int32(0), jnp.arange(N_SEQ, dtype=jnp.int32))
    tree_f = tree.astype(jnp.float32)
    tree_keys = tree_f[:, 0].reshape(ROWS, KVH, DH)
    tree_vals = tree_f[:, 1].reshape(ROWS, KVH, DH)
    tree_scores = jnp.einsum('rkgd,nkd->rkgn', heads, tree_keys) * scale
    linked = ancestry(parents)[:, None, None, :]
    tree_top = lax.optimization_barrier(jnp.max(jnp.where(linked, tree_scores, NEG), axis=-1))
    tree_weights = jnp.where(linked, jnp.exp(tree_scores - tree_top[..., None]), 0.0)
    tree_total = lax.optimization_barrier(jnp.sum(tree_weights, axis=-1))
    tree_out = jnp.einsum('rkgn,nkd->rkgd', rounded(tree_weights), tree_vals)
    peak = jnp.maximum(lax.optimization_barrier(jnp.max(tops, axis=0)), tree_top)
    factor = jnp.exp(tops - peak[None])
    tree_factor = jnp.exp(tree_top - peak)
    numer = lax.optimization_barrier(jnp.sum(factor[..., None] * outs, axis=0)) + tree_factor[..., None] * tree_out
    denom = lax.optimization_barrier(jnp.sum(factor * totals, axis=0)) + tree_factor * tree_total
    return (numer / denom[..., None]).astype(jnp.bfloat16).reshape(ROWS, HQ * DH)

def route(ids, gates):
    table = jnp.arange(EXPERTS, dtype=jnp.int32)
    hits = ids[:, :, None] == table[None, None, :]
    choose = lax.optimization_barrier(jnp.sum(hits.astype(jnp.int32), axis=1))
    weight = lax.optimization_barrier(jnp.sum(jnp.where(hits, gates.astype(jnp.float32)[:, :, None], 0.0), axis=1))
    slot = jnp.cumsum(choose, axis=0) - choose
    return (choose, weight, slot)

def reference(queries, kv_cache, tree_kv, context_lengths, tree_parents, resid, out_weight, norm_gain, expert_ids, gate_weights, w_gate, w_up, w_down):

    def one_request(packed):
        query, cache, tree, length, parents, base = packed
        attention = attend(query, cache, tree, length, parents)
        attended = jnp.dot(attention, out_weight, preferred_element_type=jnp.float32).astype(jnp.bfloat16)
        midf = rounded(base.astype(jnp.float32) + attended.astype(jnp.float32))
        factor = lax.rsqrt(lax.optimization_barrier(jnp.mean(midf * midf, axis=-1, keepdims=True)) + EPS)
        normed = (midf * factor * norm_gain.astype(jnp.float32)).astype(jnp.bfloat16)
        return (attended, normed)
    attended, normed = lax.map(one_request, (queries, kv_cache, tree_kv, context_lengths, tree_parents, resid))
    choose, weight, slot = jax.vmap(route)(expert_ids, gate_weights)
    normed_f = normed.astype(jnp.float32)
    seats = jnp.arange(CAP, dtype=jnp.int32)

    def expert_step(total, expert):
        picked = jnp.arange(EXPERTS, dtype=jnp.int32) == expert
        col_choose = lax.optimization_barrier(jnp.sum(jnp.where(picked, choose, 0), axis=-1))
        col_slot = lax.optimization_barrier(jnp.sum(jnp.where(picked, slot, 0), axis=-1))
        col_weight = lax.optimization_barrier(jnp.sum(jnp.where(picked, weight, 0.0), axis=-1))
        select = ((col_choose[:, None, :] > 0) & (col_slot[:, None, :] == seats[None, :, None])).astype(jnp.float32)
        rows = jnp.einsum('bci,bid->bcd', select, normed_f)
        rates = jnp.einsum('bci,bi->bc', select, col_weight)
        first = (expert * SPLIT).astype(jnp.int32)
        wg = lax.dynamic_slice_in_dim(w_gate, first, SPLIT, 0).astype(jnp.float32)
        wu = lax.dynamic_slice_in_dim(w_up, first, SPLIT, 0).astype(jnp.float32)
        wd = lax.dynamic_slice_in_dim(w_down, first, SPLIT, 0).astype(jnp.float32)
        gate = jnp.einsum('bcd,kdh->bckh', rows, wg)
        up = jnp.einsum('bcd,kdh->bckh', rows, wu)
        hidden = rounded(jax.nn.silu(gate) * up * rates[:, :, None, None])
        part = rounded(jnp.einsum('bckh,khd->bckd', hidden, wd))
        return (total + jnp.einsum('bci,bckd->bid', select, part), None)
    start = jnp.zeros((REQUESTS, ROWS, D), jnp.float32)
    total, _ = lax.scan(expert_step, start, jnp.arange(EXPERTS, dtype=jnp.int32))
    return (attended, total.astype(jnp.bfloat16))
```

```python
import functools

import jax
import jax.numpy as jnp
from jax import lax
from jax.experimental import pallas as pl
from jax.experimental.pallas import tpu as pltpu
from jax.sharding import PartitionSpec as P

DH = 128
HQ = 32
KVH = 2
EXPERTS = 64
CAP = 32
SPLIT = 8


NEG = -1e30
EPS = 1e-06
CHUNKS = 2
VMEM_LIMIT = 48 * 1024 * 1024


def hop(value, mask):
    count = lax.axis_size("seq")
    return lax.ppermute(value, "seq", [(i, i ^ mask) for i in range(count)])


def turn(value, step):
    count = lax.axis_size("req")
    return lax.ppermute(value, "req", [(i, (i + step) % count) for i in range(count)])


def block_order(parts):
    bits = parts.bit_length() - 1
    return [int(format(p, "b").zfill(bits)[::-1], 2) if bits else 0 for p in range(parts)]


def ancestry(parents):
    count = parents.shape[0]
    node = jnp.arange(count, dtype=jnp.int32)
    linked = (parents[:, None] == node[None, :]) | (node[:, None] == node[None, :])
    reach = linked.astype(jnp.bfloat16)
    hops = 1
    while hops < count:
        paths = jnp.dot(reach, reach, preferred_element_type=jnp.float32)
        reach = jnp.minimum(paths, 1.0).astype(jnp.bfloat16)
        hops = hops * 2
    return reach


def attend_kernel(parts, mine, valid_ref, q_ref, mask_ref, tree_ref, *refs):
    kv_refs = refs[:parts]
    w_ref, keep_ref, send_ref = refs[parts : parts + 3]
    rows = q_ref.shape[0]
    scale = DH ** (-0.5)
    q = jnp.concatenate([q_ref[:, a * DH : (a + 1) * DH] for a in range(mine)], axis=0)

    def scores(keys):
        return (
            lax.dot_general(q, keys, (((1,), (1,)), ((), ())), preferred_element_type=jnp.float32)
            * scale
        )

    linked = jnp.concatenate([mask_ref[...]] * mine, axis=0) > 0.5
    s = jnp.where(linked, scores(tree_ref[:, :DH]), NEG)
    top = jnp.max(s, axis=-1, keepdims=True)
    weights = jnp.exp(s - top)
    total = jnp.sum(weights, axis=-1, keepdims=True)
    out = jnp.dot(
        weights.astype(jnp.bfloat16), tree_ref[:, DH:], preferred_element_type=jnp.float32
    )
    for part in range(parts):
        kv = kv_refs[part]
        s = scores(kv[:, :DH])
        place = lax.broadcasted_iota(jnp.int32, s.shape, 1)
        s = jnp.where(place < valid_ref[part], s, NEG)
        peak = jnp.maximum(top, jnp.max(s, axis=-1, keepdims=True))
        weights = jnp.exp(s - peak)
        fade = jnp.exp(top - peak)
        total = total * fade + jnp.sum(weights, axis=-1, keepdims=True)
        out = out * fade + jnp.dot(
            weights.astype(jnp.bfloat16), kv[:, DH:], preferred_element_type=jnp.float32
        )
        top = peak
    attention = (out / total).astype(jnp.bfloat16)
    attention = jnp.concatenate(
        [attention[a * rows : (a + 1) * rows] for a in range(mine)], axis=1
    )
    half = rows // 2
    width = w_ref.shape[1]
    tile = min(width, 1024)
    for first in range(0, width, tile):
        piece = jnp.dot(
            attention, w_ref[:, first : first + tile], preferred_element_type=jnp.float32
        ).astype(jnp.bfloat16)
        keep_ref[:, first : first + tile] = piece[:half]
        send_ref[:, first : first + tile] = piece[half:]


def attend(valid, q, mask, tree, blocks, w):
    parts = len(blocks)
    rows, mine = q.shape[0], q.shape[1] // DH
    span = blocks[0].shape[0]
    full = pl.BlockSpec(memory_space=pltpu.VMEM)
    out = jax.ShapeDtypeStruct((rows // 2, w.shape[1]), jnp.bfloat16)
    reach = rows + parts * span
    return pl.pallas_call(
        functools.partial(attend_kernel, parts, mine),
        out_shape=(out, out),
        in_specs=[pl.BlockSpec(memory_space=pltpu.SMEM)] + [full] * (parts + 4),
        out_specs=(full, full),
        compiler_params=pltpu.CompilerParams(vmem_limit_bytes=VMEM_LIMIT),
        cost_estimate=pl.CostEstimate(
            flops=4 * rows * mine * DH * reach + 2 * rows * mine * DH * w.shape[1],
            bytes_accessed=2 * w.size + 4 * DH * reach + 2 * rows * w.shape[1],
            transcendentals=rows * mine * reach,
        ),
    )(valid, q, mask, tree, *blocks, w)


def rise_kernel(per_step, per_expert, started, sel_ref, rows_ref, wg_ref, wu_ref, *refs):
    if started:
        gate_in, up_in, gate_ref, up_ref, picked = refs
    else:
        gate_ref, up_ref, picked = refs
    step = pl.program_id(0)

    @pl.when(step == 0)
    def _():
        for e in range(picked.shape[0]):
            picked[e] = jnp.dot(
                sel_ref[e], rows_ref[...], preferred_element_type=jnp.float32
            ).astype(jnp.bfloat16)

    x = picked[(step * per_step) // per_expert]
    for k in range(per_step):
        w = jnp.concatenate([wg_ref[k], wu_ref[k]], axis=1)
        both = jnp.dot(x, w, preferred_element_type=jnp.float32)
        wide = wg_ref.shape[2]
        gate, up = both[:, :wide], both[:, wide:]
        if started:
            gate, up = gate + gate_in[k], up + up_in[k]
        gate_ref[k] = gate
        up_ref[k] = up


def rise(sel, rows, w_gate, w_up, chunk, before):
    held, depth, wide = w_gate.shape
    experts, seats, count = sel.shape
    per_expert = held // experts
    per_step = min(per_expert, 4)
    cut = rows.shape[1]
    weight = pl.BlockSpec((per_step, cut, wide), lambda j: (j, chunk, 0))
    total = pl.BlockSpec((per_step, seats, wide), lambda j: (j, 0, 0))
    shape = jax.ShapeDtypeStruct((held, seats, wide), jnp.float32)
    extra = [] if before is None else [total, total]
    return pl.pallas_call(
        functools.partial(rise_kernel, per_step, per_expert, before is not None),
        grid=(held // per_step,),
        out_shape=(shape, shape),
        in_specs=[
            pl.BlockSpec(sel.shape, lambda j: (0, 0, 0)),
            pl.BlockSpec(rows.shape, lambda j: (0, 0)),
            weight,
            weight,
        ]
        + extra,
        out_specs=(total, total),
        scratch_shapes=[pltpu.VMEM((experts, seats, cut), jnp.bfloat16)],
        compiler_params=pltpu.CompilerParams(vmem_limit_bytes=VMEM_LIMIT),
        cost_estimate=pl.CostEstimate(
            flops=4 * held * seats * cut * wide + 2 * experts * seats * count * cut,
            bytes_accessed=4 * held * cut * wide + 2 * count * cut,
            transcendentals=0,
        ),
    )(sel, rows, w_gate, w_up, *(() if before is None else before))


def fall_kernel(
    per_step, per_expert, gate_ref, up_ref, rate_ref, wd_ref, back_ref, keep_ref, send_ref, total
):
    step = pl.program_id(0)
    e = (step * per_step) // per_expert
    rate = rate_ref[e]
    acc = None
    for k in range(per_step):
        gate = gate_ref[k]
        hidden = (gate / (1.0 + jnp.exp(-gate)) * up_ref[k] * rate).astype(jnp.bfloat16)
        term = jnp.dot(hidden, wd_ref[k], preferred_element_type=jnp.float32)
        acc = term if acc is None else acc + term
    first = (step * per_step) % per_expert == 0

    @pl.when(first)
    def _():
        total[e] = acc

    @pl.when(jnp.logical_not(first))
    def _():
        total[e] += acc

    @pl.when(step == pl.num_programs(0) - 1)
    def _():
        experts, seats, cut = total.shape
        half = keep_ref.shape[0]
        flat = total[...].astype(jnp.bfloat16).reshape(experts * seats, cut)
        keep_ref[...] = jnp.dot(
            back_ref[:half], flat, preferred_element_type=jnp.float32
        ).astype(jnp.bfloat16)
        send_ref[...] = jnp.dot(
            back_ref[half:], flat, preferred_element_type=jnp.float32
        ).astype(jnp.bfloat16)


def fall(gate, up, rate, w_down, back, chunk, cut):
    held, wide, depth = w_down.shape
    experts, seats, _ = rate.shape
    count = back.shape[0]
    per_expert = held // experts
    per_step = min(per_expert, 4)
    shape = jax.ShapeDtypeStruct((count // 2, cut), jnp.bfloat16)
    whole = pl.BlockSpec((count // 2, cut), lambda j: (0, 0))
    total = pl.BlockSpec((per_step, seats, wide), lambda j: (j, 0, 0))
    return pl.pallas_call(
        functools.partial(fall_kernel, per_step, per_expert),
        grid=(held // per_step,),
        out_shape=(shape, shape),
        in_specs=[
            total,
            total,
            pl.BlockSpec(rate.shape, lambda j: (0, 0, 0)),
            pl.BlockSpec((per_step, wide, cut), lambda j: (j, 0, chunk)),
            pl.BlockSpec(back.shape, lambda j: (0, 0)),
        ],
        out_specs=(whole, whole),
        scratch_shapes=[pltpu.VMEM((experts, seats, cut), jnp.float32)],
        compiler_params=pltpu.CompilerParams(vmem_limit_bytes=VMEM_LIMIT),
        cost_estimate=pl.CostEstimate(
            flops=2 * held * seats * cut * wide + 2 * experts * seats * count * cut,
            bytes_accessed=2 * held * cut * wide + 4 * count * cut,
            transcendentals=held * seats * wide,
        ),
    )(gate, up, rate, w_down, back)


def body(
    queries,
    kv_cache,
    tree_kv,
    context_lengths,
    tree_parents,
    resid,
    out_weight,
    norm_gain,
    expert_ids,
    gate_weights,
    w_gate,
    w_up,
    w_down,
):
    here = lax.axis_index("seq")
    there = lax.axis_index("req")
    parts = lax.axis_size("seq")
    groups = lax.axis_size("req")
    bits = parts.bit_length() - 1
    order = block_order(parts)
    near = order[: parts // 2]
    own = queries.shape[1]
    rows = own * parts
    depth = resid.shape[2]

    table = jnp.concatenate(
        [expert_ids[0].astype(jnp.bfloat16), gate_weights[0]], axis=1
    )
    tables = [table] + [turn(table, d) for d in range(1, groups)]

    span = kv_cache.shape[1]
    share = parts // KVH
    lane = kv_cache[0]
    heads = [
        lane[:, :, h * DH : (h + 1) * DH].reshape(span, 2 * DH) for h in range(KVH)
    ]

    def head_of(device):
        pick = heads[0]
        for h in range(1, KVH):
            pick = jnp.where(device // share == h, heads[h], pick)
        return pick

    half = [head_of(here ^ mask) if mask == 0 else None for mask in near]
    same = half[0]
    other = head_of(here ^ (parts // 2))
    half = [same] + [hop(other if mask & (parts // 2) else same, mask) for mask in near[1:]]
    blocks = half + [hop(piece, 1) for piece in half]
    valid = context_lengths[0] - jnp.stack([(here ^ mask) * span for mask in order])

    q = queries[0]
    tree_heads = [
        tree_kv[0][:, :, h * DH : (h + 1) * DH].reshape(own, 2 * DH) for h in range(KVH)
    ]
    top_bit = (here >> (bits - 1)) & 1
    tree = jnp.where(top_bit == 1, tree_heads[1], tree_heads[0])
    tree_send = jnp.where(top_bit == 1, tree_heads[0], tree_heads[1])
    for bit in range(bits - 1, -1, -1):
        wide = q.shape[1] // 2
        upper = ((here >> bit) & 1) == 1
        low, high = q[:, :wide], q[:, wide:]
        kept = jnp.where(upper, high, low)
        packed = jnp.concatenate([jnp.where(upper, low, high), tree_send], axis=1)
        got = hop(packed, 1 << bit)
        q = jnp.concatenate([kept, got[:, :wide]], axis=0)
        tree = jnp.concatenate([tree, got[:, wide:]], axis=0)
        tree_send = tree

    wanted = jnp.stack([here ^ mask for mask in order])
    swap = wanted[:, None] == jnp.arange(parts, dtype=jnp.int32)[None, :]

    def placed(values):
        cut = values.reshape((parts, own) + values.shape[1:])
        tail = (1,) * (cut.ndim - 1)
        moved = jnp.sum(
            jnp.where(swap.reshape((parts, parts) + tail), cut[None].astype(jnp.float32), 0.0), axis=1
        )
        return moved.reshape((parts, own) + values.shape[1:])

    reach = ancestry(tree_parents[0])
    across = placed(reach).reshape(rows, rows).T
    linked = placed(across).reshape(rows, rows).T.astype(jnp.bfloat16)

    keep, send = attend(valid.astype(jnp.int32), q, linked, tree, blocks, out_weight)

    got = hop(send, 1)
    pair = [
        keep[i * own : (i + 1) * own].astype(jnp.float32)
        + got[i * own : (i + 1) * own].astype(jnp.float32)
        for i in range(len(near))
    ]
    terms = [pair[0]] + [
        hop(pair[i].astype(jnp.bfloat16), near[i]).astype(jnp.float32)
        for i in range(1, len(near))
    ]
    attended = sum(terms[1:], terms[0]).astype(jnp.bfloat16)
    mid = (resid[0].astype(jnp.float32) + attended.astype(jnp.float32)).astype(jnp.bfloat16)
    midf = lax.optimization_barrier(mid).astype(jnp.float32)
    factor = lax.rsqrt(jnp.mean(midf * midf, axis=-1, keepdims=True) + EPS)
    normed = (midf * factor * norm_gain.astype(jnp.float32)).astype(jnp.bfloat16)

    held = w_gate.shape[0]
    experts = max(1, held // SPLIT)
    first = ((there * parts + here) * held) // SPLIT
    count = groups * rows
    seats = groups * CAP
    listing = jnp.stack([placed(t) for t in tables], axis=1).reshape(count, -1)
    topk = listing.shape[1] // 2
    mine = (first + jnp.arange(experts, dtype=jnp.int32)).astype(jnp.float32)
    hits = listing[None, :, :topk] == mine[:, None, None]
    chosen = jnp.sum(hits.astype(jnp.float32), axis=2)
    weight = jnp.sum(jnp.where(hits, listing[None, :, topk:], 0.0), axis=2)
    index = jnp.arange(count, dtype=jnp.int32)
    before = (index[:, None] < index[None, :]).astype(jnp.bfloat16)
    seat = jnp.dot(chosen.astype(jnp.bfloat16), before, preferred_element_type=jnp.float32)
    seat = jnp.where(chosen > 0.5, seat.astype(jnp.int32), -1)
    select = seat[:, None, :] == jnp.arange(seats, dtype=jnp.int32)[None, :, None]
    sel = select.astype(jnp.bfloat16)
    rate = jnp.sum(jnp.where(select, weight[:, None, :], 0.0), axis=2)[..., None]
    back = sel.reshape(experts * seats, count).T

    cut = depth // CHUNKS
    sums = None
    for chunk in range(CHUNKS):
        piece = normed[:, chunk * cut : (chunk + 1) * cut]
        stack = jnp.concatenate([piece] + [turn(piece, d) for d in range(1, groups)], axis=0)
        plane = [stack] + [hop(stack, mask) for mask in near[1:]]
        full = jnp.concatenate(plane + [hop(p, 1) for p in plane], axis=0)
        sums = rise(sel, full, w_gate, w_up, chunk, sums)

    pieces = []
    for chunk in range(CHUNKS):
        keep, send = fall(sums[0], sums[1], rate, w_down, back, chunk, cut)
        got = hop(send, 1)
        size = groups * own
        pair = [
            keep[i * size : (i + 1) * size].astype(jnp.float32)
            + got[i * size : (i + 1) * size].astype(jnp.float32)
            for i in range(len(near))
        ]
        terms = [pair[0]] + [
            hop(pair[i].astype(jnp.bfloat16), near[i]).astype(jnp.float32)
            for i in range(1, len(near))
        ]
        flat = sum(terms[1:], terms[0])
        result = flat[:own]
        for d in range(1, groups):
            result = result + turn(
                flat[d * own : (d + 1) * own].astype(jnp.bfloat16), -d
            ).astype(jnp.float32)
        pieces.append(result.astype(jnp.bfloat16))
    return (attended[None], jnp.concatenate(pieces, axis=1)[None])


def solution(mesh):
    placed = (
        P("req", "seq", None),
        P("req", "seq", None, None),
        P("req", "seq", None, None),
        P("req"),
        P("req", None),
        P("req", "seq", None),
        P("seq", None),
        P(),
        P("req", None, None),
        P("req", None, None),
        P(("req", "seq"), None, None),
        P(("req", "seq"), None, None),
        P(("req", "seq"), None, None),
    )
    return jax.shard_map(
        body,
        mesh=mesh,
        in_specs=placed,
        out_specs=(P("req", "seq", None), P("req", "seq", None)),
        check_vma=False,
    )
```

```python
import functools

import jax
import jax.numpy as jnp
from jax import lax
from jax.experimental import pallas as pl
from jax.experimental.pallas import tpu as pltpu
from jax.sharding import PartitionSpec as P

DH = 128
HQ = 32
KVH = 2
EXPERTS = 64
CAP = 32
SPLIT = 8


NEG = -1e30
EPS = 1e-06
RISE_LIMIT = 34 * 1024 * 1024
FALL_LIMIT = 37 * 1024 * 1024
ATTEND_LIMIT = 48 * 1024 * 1024
READY = 8
LOG2E = 1.4426950408889634


def hop(value, mask):
    count = lax.axis_size("seq")
    return lax.ppermute(value, "seq", [(i, i ^ mask) for i in range(count)])


def turn(value, step):
    count = lax.axis_size("req")
    return lax.ppermute(value, "req", [(i, i ^ step) for i in range(count)])


def block_order(parts):
    bits = parts.bit_length() - 1
    return [int(format(p, "b").zfill(bits)[::-1], 2) if bits else 0 for p in range(parts)]


def ancestry(parents):
    count = parents.shape[0]
    node = jnp.arange(count, dtype=jnp.int32)
    linked = (parents[:, None] == node[None, :]) | (node[:, None] == node[None, :])
    reach = linked.astype(jnp.bfloat16)
    hops = 1
    while hops < count:
        paths = jnp.dot(reach, reach, preferred_element_type=jnp.float32)
        reach = jnp.minimum(paths, 1.0).astype(jnp.bfloat16)
        hops = hops * 2
    return reach


def attend_kernel(parts, mine, valid_ref, perm_ref, packed_ref, mask_ref, *refs):
    kv_refs = refs[:parts]
    w_any, keep_ref, send_ref, w_ref, sem = refs[parts:]
    copy = pltpu.make_async_copy(w_any, w_ref, sem)
    copy.start()
    rows = packed_ref.shape[0]
    lanes = mine * DH
    scale = DH ** (-0.5) * LOG2E
    perm = perm_ref[...]
    q = jnp.dot(perm, packed_ref[:, :lanes], preferred_element_type=jnp.float32).astype(jnp.bfloat16)
    q = jnp.concatenate([q[:, a * DH : (a + 1) * DH] for a in range(mine)], axis=0)

    def scores(keys):
        return (
            lax.dot_general(q, keys, (((1,), (1,)), ((), ())), preferred_element_type=jnp.float32)
            * scale
        )

    mask = jnp.dot(perm, mask_ref[...], preferred_element_type=jnp.float32)
    linked = jnp.concatenate([mask] * mine, axis=0) > 0.5
    s = jnp.where(linked, scores(packed_ref[:, lanes : lanes + DH]), NEG)
    top = jnp.max(s, axis=-1, keepdims=True)
    weights = jnp.exp2(s - top)
    total = jnp.sum(weights, axis=-1, keepdims=True)
    out = jnp.dot(
        weights.astype(jnp.bfloat16),
        packed_ref[:, lanes + DH :],
        preferred_element_type=jnp.float32,
    )
    for part in range(parts):
        kv = kv_refs[part]
        place = lax.broadcasted_iota(jnp.int32, (1, kv.shape[0]), 1)
        bias = jnp.where(place < valid_ref[part], 0.0, NEG)
        s = scores(kv[:, :DH]) + bias
        peak = jnp.maximum(top, jnp.max(s, axis=-1, keepdims=True))
        weights = jnp.exp2(s - peak)
        fade = jnp.exp2(top - peak)
        total = total * fade + jnp.sum(weights, axis=-1, keepdims=True)
        out = out * fade + jnp.dot(
            weights.astype(jnp.bfloat16), kv[:, DH:], preferred_element_type=jnp.float32
        )
        top = peak
    attention = (out / total).astype(jnp.bfloat16)
    attention = jnp.concatenate(
        [attention[a * rows : (a + 1) * rows] for a in range(mine)], axis=1
    )
    copy.wait()
    half = rows // 2
    width = w_ref.shape[1]
    tile = min(width, 1024)
    for first in range(0, width, tile):
        piece = jnp.dot(
            attention, w_ref[:, first : first + tile], preferred_element_type=jnp.float32
        ).astype(jnp.bfloat16)
        keep_ref[:, first : first + tile] = piece[:half]
        send_ref[:, first : first + tile] = piece[half:]


def attend(valid, perm, packed, mask, blocks, w):
    parts = len(blocks)
    rows, mine = packed.shape[0], (packed.shape[1] - 2 * DH) // DH
    span = blocks[0].shape[0]
    full = pl.BlockSpec(memory_space=pltpu.VMEM)
    out = jax.ShapeDtypeStruct((rows // 2, w.shape[1]), jnp.bfloat16)
    reach = rows + parts * span
    return pl.pallas_call(
        functools.partial(attend_kernel, parts, mine),
        out_shape=(out, out),
        in_specs=[pl.BlockSpec(memory_space=pltpu.SMEM)]
        + [full] * (parts + 3)
        + [pl.BlockSpec(memory_space=pltpu.HBM)],
        out_specs=(full, full),
        scratch_shapes=[pltpu.VMEM(w.shape, w.dtype), pltpu.SemaphoreType.DMA],
        compiler_params=pltpu.CompilerParams(vmem_limit_bytes=ATTEND_LIMIT),
        cost_estimate=pl.CostEstimate(
            flops=4 * rows * mine * DH * reach + 2 * rows * mine * DH * w.shape[1],
            bytes_accessed=2 * w.size + 4 * DH * reach + 2 * rows * w.shape[1],
            transcendentals=rows * mine * reach,
        ),
    )(valid, perm, packed, mask, *blocks, w)


def seat_rows(first_ref, topk, table, back_ref, experts, seats):
    count = table.shape[0]
    block = min(count, 256)
    lane = lax.broadcasted_iota(jnp.int32, (count, DH), 1)
    hits = []
    spread = jnp.zeros((count, DH), jnp.float32)
    for e in range(experts):
        named = (first_ref[0] + e).astype(jnp.float32)
        match = jnp.where((table == named) & (lane < topk), 1.0, 0.0)
        hits.append(jnp.max(match, axis=1, keepdims=True))
        spread = spread + jnp.where(lane == e, hits[e], 0.0)
    ahead = lax.broadcasted_iota(jnp.int32, (block, block), 0) > lax.broadcasted_iota(
        jnp.int32, (block, block), 1
    )
    ahead = jnp.where(ahead, 1.0, 0.0).astype(jnp.bfloat16)
    place = lax.broadcasted_iota(jnp.int32, (block, seats), 1).astype(jnp.float32)
    carry = jnp.zeros((1, DH), jnp.float32)
    for at in range(0, count, block):
        here = spread[at : at + block]
        before = carry + jnp.dot(
            ahead, here.astype(jnp.bfloat16), preferred_element_type=jnp.float32
        )
        carry = carry + jnp.sum(here, axis=0, keepdims=True)
        for e in range(experts):
            seat = jnp.sum(jnp.where(lane[:block] == e, before, 0.0), axis=1, keepdims=True)
            taken = (hits[e][at : at + block] > 0.5) & (seat == place)
            back_ref[at : at + block, e * seats : (e + 1) * seats] = jnp.where(
                taken, 1.0, 0.0
            ).astype(jnp.bfloat16)


def pick_rows(back_ref, rows, first, width):
    return lax.dot_general(
        back_ref[...],
        rows[:, first : first + width],
        (((0,), (0,)), ((), ())),
        preferred_element_type=jnp.float32,
    )


def expert_kernel(pieces, experts, seats, topk, chunk, *refs):
    refs = list(refs)

    def take(count):
        out = refs[:count]
        del refs[:count]
        return out

    part_refs = take(pieces)
    wg_any, wu_any = take(2)
    if chunk == 0:
        first_ref, wd_any = take(2)
        gate_ref, up_ref, back_ref, rate_ref, ready_ref = take(5)
    else:
        gate_in, up_in, back_ref, rate_ref, ready_ref, wd_any = take(6)
        outs = take(4)
    rows, picked, wg, wu, part_sem, gate_sem, up_sem = take(7)
    held, cut, wide = wg.shape
    per_expert = held // experts
    size = rows.shape[0] // pieces
    moves = [
        pltpu.make_async_copy(ref, rows.at[pl.ds(i * size, size)], part_sem.at[i])
        for i, ref in enumerate(part_refs)
    ]
    for move in moves:
        move.start()
    first = chunk * cut

    def weight_moves(p):
        return (
            pltpu.make_async_copy(wg_any.at[p, pl.ds(first, cut)], wg.at[p], gate_sem.at[p]),
            pltpu.make_async_copy(wu_any.at[p, pl.ds(first, cut)], wu.at[p], up_sem.at[p]),
        )

    for p in range(held):
        for move in weight_moves(p):
            move.start()
    if chunk == 0:
        (ready_sem,) = take(1)
        early = [
            pltpu.make_async_copy(wd_any.at[p], ready_ref.at[p], ready_sem.at[p])
            for p in range(ready_ref.shape[0])
        ]
        for move in early:
            move.start()
    else:
        wd, hidden, flat, down_sem = take(4)

        ready = ready_ref.shape[0]

        def down_move(p):
            place = pl.ds((p - ready) * wide, wide)
            return pltpu.make_async_copy(wd_any.at[p], wd.at[place], down_sem.at[p - ready])

        for p in range(ready, held):
            down_move(p).start()
    for move in moves:
        move.wait()
    if chunk == 0:
        seat_rows(first_ref, topk, rows[:, cut:].astype(jnp.float32), back_ref, experts, seats)
        meta = pick_rows(back_ref, rows, cut, DH)
        lane = lax.broadcasted_iota(jnp.int32, (seats, DH), 1)
        for e in range(experts):
            named = (first_ref[0] + e).astype(jnp.float32)
            own = meta[e * seats : (e + 1) * seats]
            gates = pltpu.roll(own, DH - topk, 1)
            rate_ref[e] = jnp.sum(
                jnp.where((own == named) & (lane < topk), gates, 0.0), axis=1, keepdims=True
            )
    tile = 512 if cut % 512 == 0 else cut
    for c in range(0, cut, tile):
        picked[:, c : c + tile] = pick_rows(back_ref, rows, c, tile).astype(jnp.bfloat16)
    for e in range(experts):

        def panel(k, carry, e=e):
            p = e * per_expert + k
            for move in weight_moves(p):
                move.wait()
            w = jnp.concatenate([wg[p], wu[p]], axis=1)
            both = jnp.dot(
                picked[e * seats : (e + 1) * seats], w, preferred_element_type=jnp.float32
            )
            gate, up = both[:, :wide], both[:, wide:]
            if chunk:
                gate, up = gate + gate_in[p], up + up_in[p]
                value = gate / (1.0 + jnp.exp(-gate)) * up * rate_ref[e]
                place = pl.ds(pl.multiple_of(k * wide, wide), wide)
                hidden[e * seats : (e + 1) * seats, place] = value.astype(jnp.bfloat16)
            else:
                gate_ref[p] = gate
                up_ref[p] = up
            return carry

        lax.fori_loop(0, per_expert, panel, 0)
    if chunk == 0:
        for move in early:
            move.wait()
        return
    deep = per_expert * wide
    depth = flat.shape[1]
    for e in range(experts):
        low, high = e * per_expert, (e + 1) * per_expert
        for p in range(max(low, ready), high):
            down_move(p).wait()
        split = min(max(ready, low), high)
        for c in range(0, depth, tile):
            total = None
            if split > low:
                total = jnp.dot(
                    hidden[e * seats : (e + 1) * seats, : (split - low) * wide],
                    ready_ref[low:split, :, c : c + tile].reshape(-1, tile),
                    preferred_element_type=jnp.float32,
                )
            if split < high:
                rest = jnp.dot(
                    hidden[e * seats : (e + 1) * seats, (split - low) * wide :],
                    wd[(split - ready) * wide : (high - ready) * wide, c : c + tile],
                    preferred_element_type=jnp.float32,
                )
                total = rest if total is None else total + rest
            flat[e * seats : (e + 1) * seats, c : c + tile] = total.astype(jnp.bfloat16)
    for c in range(0, depth, tile):
        moved = jnp.dot(
            back_ref[...], flat[:, c : c + tile], preferred_element_type=jnp.float32
        ).astype(jnp.bfloat16)
        half = moved.shape[0] // 2
        keep_ref, send_ref = outs[2 * (c // cut)], outs[2 * (c // cut) + 1]
        at = c % cut
        keep_ref[:, at : at + tile] = moved[:half]
        send_ref[:, at : at + tile] = moved[half:]


def expert_call(rows, w_gate, w_up, chunk, cut, topk, experts, seats, first=None, sums=None, w_down=None):
    held, depth, wide = w_gate.shape
    count = rows[0].shape[0] * len(rows)
    full = pl.BlockSpec(memory_space=pltpu.VMEM)
    anywhere = pl.BlockSpec(memory_space=pl.ANY)
    far = pl.BlockSpec(memory_space=pltpu.HBM)
    deep = held // experts * wide
    args = [*rows, w_gate, w_up]
    in_specs = [anywhere] * len(rows) + [far, far]
    scratch = [
        pltpu.VMEM((count, rows[0].shape[1]), jnp.bfloat16),
        pltpu.VMEM((experts * seats, cut), jnp.bfloat16),
        pltpu.VMEM((held, cut, wide), jnp.bfloat16),
        pltpu.VMEM((held, cut, wide), jnp.bfloat16),
        pltpu.SemaphoreType.DMA((len(rows),)),
        pltpu.SemaphoreType.DMA((held,)),
        pltpu.SemaphoreType.DMA((held,)),
    ]
    flops = 4 * held * seats * cut * wide + 2 * experts * seats * count * cut
    moved = 4 * held * cut * wide + 2 * count * cut
    if chunk == 0:
        early = max(1, held * READY // 16)
        args += [first, w_down]
        in_specs += [pl.BlockSpec(memory_space=pltpu.SMEM), far]
        outs = [jax.ShapeDtypeStruct((held, seats, wide), jnp.float32)] * 2 + [
            jax.ShapeDtypeStruct((count, experts * seats), jnp.bfloat16),
            jax.ShapeDtypeStruct((experts, seats, 1), jnp.float32),
            jax.ShapeDtypeStruct((early, wide, depth), jnp.bfloat16),
        ]
        scratch += [pltpu.SemaphoreType.DMA((early,))]
        moved += 2 * early * wide * depth
    else:
        ready = sums[4]
        args += [*sums, w_down]
        in_specs += [full] * 5 + [far]
        outs = [jax.ShapeDtypeStruct((count // 2, cut), jnp.bfloat16)] * 4
        scratch += [
            pltpu.VMEM((max(1, held - ready.shape[0]) * wide, depth), jnp.bfloat16),
            pltpu.VMEM((experts * seats, deep), jnp.bfloat16),
            pltpu.VMEM((experts * seats, depth), jnp.bfloat16),
            pltpu.SemaphoreType.DMA((max(1, held - ready.shape[0]),)),
        ]
        flops += 2 * held * seats * depth * wide + 2 * experts * seats * count * depth
        moved += 2 * held * depth * wide
    return pl.pallas_call(
        functools.partial(expert_kernel, len(rows), experts, seats, topk, chunk),
        out_shape=tuple(outs),
        in_specs=in_specs,
        out_specs=tuple([full] * len(outs)),
        scratch_shapes=scratch,
        compiler_params=pltpu.CompilerParams(vmem_limit_bytes=RISE_LIMIT if chunk == 0 else FALL_LIMIT),
        cost_estimate=pl.CostEstimate(flops=flops, bytes_accessed=moved, transcendentals=0),
    )(*args)


def body(
    queries,
    kv_cache,
    tree_kv,
    context_lengths,
    tree_parents,
    resid,
    out_weight,
    norm_gain,
    expert_ids,
    gate_weights,
    w_gate,
    w_up,
    w_down,
):
    here = lax.axis_index("seq")
    there = lax.axis_index("req")
    parts = lax.axis_size("seq")
    groups = lax.axis_size("req")
    bits = parts.bit_length() - 1
    order = block_order(parts)
    near = order[: parts // 2]
    own = queries.shape[1]
    rows = own * parts
    depth = resid.shape[2]

    span = kv_cache.shape[1]
    share = parts // KVH
    lane = kv_cache[0]
    heads = [
        lane[:, :, h * DH : (h + 1) * DH].reshape(span, 2 * DH) for h in range(KVH)
    ]

    def head_of(device):
        pick = heads[0]
        for h in range(1, KVH):
            pick = jnp.where(device // share == h, heads[h], pick)
        return pick

    half = [head_of(here ^ mask) if mask == 0 else None for mask in near]
    same = half[0]
    other = head_of(here ^ (parts // 2))
    half = [same] + [hop(other if mask & (parts // 2) else same, mask) for mask in near[1:]]
    valid = context_lengths[0] - jnp.stack([(here ^ mask) * span for mask in order])

    mine = HQ // parts
    tree_heads = [
        tree_kv[0][:, :, h * DH : (h + 1) * DH].reshape(own, 2 * DH) for h in range(KVH)
    ]
    asked = jnp.transpose(queries[0].reshape(own, parts, mine * DH), (1, 0, 2))
    trees = jnp.stack(tree_heads)[:, None]
    trees = jnp.broadcast_to(trees, (KVH, share, own, 2 * DH)).reshape(parts, own, 2 * DH)
    packed = jnp.concatenate([asked, trees], axis=2)
    packed = lax.all_to_all(packed, "seq", split_axis=0, concat_axis=0, tiled=True)
    packed = packed.reshape(rows, -1)

    wanted = jnp.stack([here ^ mask for mask in order])
    wanted = (wanted[:, None] * own + jnp.arange(own, dtype=jnp.int32)[None, :]).reshape(rows)
    perm = (wanted[:, None] == jnp.arange(rows, dtype=jnp.int32)[None, :]).astype(jnp.bfloat16)

    linked = ancestry(tree_parents[0])
    blocks = half + [hop(piece, 1) for piece in half]
    keep, send = attend(valid.astype(jnp.int32), perm, packed, linked, blocks, out_weight)

    got = hop(send, 1)
    pair = [
        keep[i * own : (i + 1) * own].astype(jnp.float32)
        + got[i * own : (i + 1) * own].astype(jnp.float32)
        for i in range(len(near))
    ]
    terms = [pair[0]] + [
        hop(pair[i].astype(jnp.bfloat16), near[i]).astype(jnp.float32)
        for i in range(1, len(near))
    ]
    attended = sum(terms[1:], terms[0]).astype(jnp.bfloat16)
    mid = (resid[0].astype(jnp.float32) + attended.astype(jnp.float32)).astype(jnp.bfloat16)
    midf = lax.optimization_barrier(mid).astype(jnp.float32)
    factor = lax.rsqrt(jnp.mean(midf * midf, axis=-1, keepdims=True) + EPS)
    normed = (midf * factor * norm_gain.astype(jnp.float32)).astype(jnp.bfloat16)

    table = jnp.concatenate(
        [expert_ids[0].astype(jnp.bfloat16), gate_weights[0]], axis=1
    )
    table = lax.dynamic_slice_in_dim(table, here * own, own, 0)
    topk = expert_ids.shape[2]
    table = jnp.pad(table, ((0, 0), (0, DH - 2 * topk)))
    held = w_gate.shape[0]
    experts = max(1, held // SPLIT)
    first = (((there * parts + here) * held) // SPLIT).astype(jnp.int32).reshape(1)
    seats = groups * CAP

    cut = depth // 2
    planes = []
    for chunk in range(2):
        piece = normed[:, chunk * cut : (chunk + 1) * cut]
        if chunk == 0:
            piece = jnp.concatenate([piece, table], axis=1)
        stack = jnp.concatenate([piece] + [turn(piece, d) for d in range(1, groups)], axis=0)
        planes.append([stack] + [hop(stack, mask) for mask in near[1:]])
    full = planes[0] + [hop(p, 1) for p in planes[0]]
    sums = expert_call(full, w_gate, w_up, 0, cut, topk, experts, seats, first=first, w_down=w_down)
    *plane, gate = lax.optimization_barrier((*planes[1], sums[0]))
    full = plane + [hop(p, 1) for p in plane]
    keep0, send0, keep1, send1 = expert_call(
        full, w_gate, w_up, 1, cut, topk, experts, seats, sums=(gate, *sums[1:]), w_down=w_down
    )

    size = groups * own

    def home(keep, got):
        pair = [
            keep[i * size : (i + 1) * size].astype(jnp.float32)
            + got[i * size : (i + 1) * size].astype(jnp.float32)
            for i in range(len(near))
        ]
        flat = pair[0]
        for i in range(1, len(near)):
            flat = flat + hop(pair[i].astype(jnp.bfloat16), near[i]).astype(jnp.float32)
        result = flat[:own]
        for d in range(1, groups):
            result = result + turn(
                flat[d * own : (d + 1) * own].astype(jnp.bfloat16), d
            ).astype(jnp.float32)
        return result.astype(jnp.bfloat16)

    got0 = hop(send0, 1)
    send1, got0 = lax.optimization_barrier((send1, got0))
    pieces = [home(keep0, got0), home(keep1, hop(send1, 1))]
    return (attended[None], jnp.concatenate(pieces, axis=1)[None])


def solution(mesh):
    placed = (
        P("req", "seq", None),
        P("req", "seq", None, None),
        P("req", "seq", None, None),
        P("req"),
        P("req", None),
        P("req", "seq", None),
        P("seq", None),
        P(),
        P("req", None, None),
        P("req", None, None),
        P(("req", "seq"), None, None),
        P(("req", "seq"), None, None),
        P(("req", "seq"), None, None),
    )
    return jax.shard_map(
        body,
        mesh=mesh,
        in_specs=placed,
        out_specs=(P("req", "seq", None), P("req", "seq", None)),
        check_vma=False,
    )
```

```python
import functools

import jax
import jax.numpy as jnp
from jax import lax
from jax.experimental import pallas as pl
from jax.experimental.pallas import tpu as pltpu
from jax.sharding import PartitionSpec as P

DH = 128
HQ = 32
KVH = 2
EXPERTS = 64
CAP = 32
SPLIT = 8


NEG = -1e30
EPS = 1e-06
RISE_LIMIT = 34 * 1024 * 1024
FALL_LIMIT = 33 * 1024 * 1024
LAST_LIMIT = 30 * 1024 * 1024
ATTEND_LIMIT = 48 * 1024 * 1024
READY = 8
LOG2E = 1.4426950408889634


def hop(value, mask):
    count = lax.axis_size("seq")
    return lax.ppermute(value, "seq", [(i, i ^ mask) for i in range(count)])


def turn(value, step):
    count = lax.axis_size("req")
    return lax.ppermute(value, "req", [(i, i ^ step) for i in range(count)])


def block_order(parts):
    bits = parts.bit_length() - 1
    return [int(format(p, "b").zfill(bits)[::-1], 2) if bits else 0 for p in range(parts)]


def ancestry(parents):
    count = parents.shape[0]
    node = jnp.arange(count, dtype=jnp.int32)
    linked = (parents[:, None] == node[None, :]) | (node[:, None] == node[None, :])
    reach = linked.astype(jnp.bfloat16)
    hops = 1
    while hops < count:
        paths = jnp.dot(reach, reach, preferred_element_type=jnp.float32)
        reach = jnp.minimum(paths, 1.0).astype(jnp.bfloat16)
        hops = hops * 2
    return reach


def weigh(weights, values):
    values = jnp.concatenate([values, jnp.ones_like(values)], axis=1)
    return jnp.dot(weights.astype(jnp.bfloat16), values, preferred_element_type=jnp.float32)


def attend_kernel(parts, mine, valid_ref, perm_ref, packed_ref, mask_ref, *refs):
    kv_refs = refs[:parts]
    w_any, keep_ref, send_ref, w_ref, sem = refs[parts:]
    copy = pltpu.make_async_copy(w_any, w_ref, sem)
    copy.start()
    rows = packed_ref.shape[0]
    lanes = mine * DH
    scale = DH ** (-0.5) * LOG2E
    perm = perm_ref[...]
    q = jnp.dot(perm, packed_ref[:, :lanes], preferred_element_type=jnp.float32).astype(jnp.bfloat16)
    q = jnp.concatenate([q[:, a * DH : (a + 1) * DH] for a in range(mine)], axis=0)

    def scores(keys):
        return (
            lax.dot_general(q, keys, (((1,), (1,)), ((), ())), preferred_element_type=jnp.float32)
            * scale
        )

    mask = jnp.dot(perm, mask_ref[...], preferred_element_type=jnp.float32)
    linked = jnp.concatenate([mask] * mine, axis=0) > 0.5
    s = jnp.where(linked, scores(packed_ref[:, lanes : lanes + DH]), NEG)
    top = jnp.max(s, axis=-1, keepdims=True)
    out = weigh(jnp.exp2(s - top), packed_ref[:, lanes + DH :])
    for part in range(parts):
        kv = kv_refs[part]
        place = lax.broadcasted_iota(jnp.int32, (1, kv.shape[0]), 1)
        bias = jnp.where(place < valid_ref[part], 0.0, NEG)
        s = scores(kv[:, :DH]) + bias
        peak = jnp.maximum(top, jnp.max(s, axis=-1, keepdims=True))
        out = out * jnp.exp2(top - peak) + weigh(jnp.exp2(s - peak), kv[:, DH:])
        top = peak
    attention = (out[:, :DH] / out[:, DH:]).astype(jnp.bfloat16)
    attention = jnp.concatenate(
        [attention[a * rows : (a + 1) * rows] for a in range(mine)], axis=1
    )
    copy.wait()
    half = rows // 2
    width = w_ref.shape[1]
    tile = min(width, 1024)
    for first in range(0, width, tile):
        piece = jnp.dot(
            attention, w_ref[:, first : first + tile], preferred_element_type=jnp.float32
        ).astype(jnp.bfloat16)
        keep_ref[:, first : first + tile] = piece[:half]
        send_ref[:, first : first + tile] = piece[half:]


def attend(valid, perm, packed, mask, blocks, w):
    parts = len(blocks)
    rows, mine = packed.shape[0], (packed.shape[1] - 2 * DH) // DH
    span = blocks[0].shape[0]
    full = pl.BlockSpec(memory_space=pltpu.VMEM)
    out = jax.ShapeDtypeStruct((rows // 2, w.shape[1]), jnp.bfloat16)
    reach = rows + parts * span
    return pl.pallas_call(
        functools.partial(attend_kernel, parts, mine),
        out_shape=(out, out),
        in_specs=[pl.BlockSpec(memory_space=pltpu.SMEM)]
        + [full] * (parts + 3)
        + [pl.BlockSpec(memory_space=pltpu.HBM)],
        out_specs=(full, full),
        scratch_shapes=[pltpu.VMEM(w.shape, w.dtype), pltpu.SemaphoreType.DMA],
        compiler_params=pltpu.CompilerParams(vmem_limit_bytes=ATTEND_LIMIT),
        cost_estimate=pl.CostEstimate(
            flops=4 * rows * mine * DH * reach + 2 * rows * mine * DH * w.shape[1],
            bytes_accessed=2 * w.size + 4 * DH * reach + 2 * rows * w.shape[1],
            transcendentals=rows * mine * reach,
        ),
    )(valid, perm, packed, mask, *blocks, w)


def seat_rows(first_ref, topk, table, back_ref, experts, seats):
    count = table.shape[0]
    block = min(count, 256)
    lane = lax.broadcasted_iota(jnp.int32, (count, DH), 1)
    hits = []
    spread = jnp.zeros((count, DH), jnp.float32)
    for e in range(experts):
        named = (first_ref[0] + e).astype(jnp.float32)
        match = jnp.where((table == named) & (lane < topk), 1.0, 0.0)
        hits.append(jnp.max(match, axis=1, keepdims=True))
        spread = spread + jnp.where(lane == e, hits[e], 0.0)
    ahead = lax.broadcasted_iota(jnp.int32, (block, block), 0) > lax.broadcasted_iota(
        jnp.int32, (block, block), 1
    )
    ahead = jnp.where(ahead, 1.0, 0.0).astype(jnp.bfloat16)
    place = lax.broadcasted_iota(jnp.int32, (block, seats), 1).astype(jnp.float32)
    carry = jnp.zeros((1, DH), jnp.float32)
    for at in range(0, count, block):
        here = spread[at : at + block]
        before = carry + jnp.dot(
            ahead, here.astype(jnp.bfloat16), preferred_element_type=jnp.float32
        )
        carry = carry + jnp.sum(here, axis=0, keepdims=True)
        for e in range(experts):
            seat = jnp.sum(jnp.where(lane[:block] == e, before, 0.0), axis=1, keepdims=True)
            taken = (hits[e][at : at + block] > 0.5) & (seat == place)
            back_ref[at : at + block, e * seats : (e + 1) * seats] = jnp.where(
                taken, 1.0, 0.0
            ).astype(jnp.bfloat16)


def pick_rows(back_ref, rows, first, width):
    return lax.dot_general(
        back_ref[...],
        rows[:, first : first + width],
        (((0,), (0,)), ((), ())),
        preferred_element_type=jnp.float32,
    )


def expert_kernel(pieces, experts, seats, topk, chunk, *refs):
    refs = list(refs)

    def take(count):
        out = refs[:count]
        del refs[:count]
        return out

    part_refs = take(pieces)
    wg_any, wu_any = take(2)
    if chunk == 0:
        first_ref, wd_any = take(2)
        gate_ref, up_ref, back_ref, rate_ref, ready_ref = take(5)
    else:
        gate_in, up_in, back_ref, rate_ref, ready_ref, wd_any = take(6)
        outs = take(3)
        hidden = outs[2]
    rows, picked, wg, wu, part_sem, gate_sem, up_sem = take(7)
    held, cut, wide = wg.shape
    per_expert = held // experts
    size = rows.shape[0] // pieces
    moves = [
        pltpu.make_async_copy(ref, rows.at[pl.ds(i * size, size)], part_sem.at[i])
        for i, ref in enumerate(part_refs)
    ]
    for move in moves:
        move.start()
    first = chunk * cut

    def weight_moves(p):
        return (
            pltpu.make_async_copy(wg_any.at[p, pl.ds(first, cut)], wg.at[p], gate_sem.at[p]),
            pltpu.make_async_copy(wu_any.at[p, pl.ds(first, cut)], wu.at[p], up_sem.at[p]),
        )

    for p in range(held):
        for move in weight_moves(p):
            move.start()
    if chunk == 0:
        (ready_sem,) = take(1)
        early = [
            pltpu.make_async_copy(wd_any.at[p], ready_ref.at[p], ready_sem.at[p])
            for p in range(ready_ref.shape[0])
        ]
        for move in early:
            move.start()
    else:
        wd, flat, down_sem = take(3)

        ready = ready_ref.shape[0]

        def down_move(p):
            place = pl.ds((p - ready) * wide, wide)
            return pltpu.make_async_copy(
                wd_any.at[p, :, pl.ds(0, cut)], wd.at[place], down_sem.at[p - ready]
            )

        for p in range(ready, held):
            down_move(p).start()
    for move in moves:
        move.wait()
    if chunk == 0:
        seat_rows(first_ref, topk, rows[:, cut:].astype(jnp.float32), back_ref, experts, seats)
        meta = pick_rows(back_ref, rows, cut, DH)
        lane = lax.broadcasted_iota(jnp.int32, (seats, DH), 1)
        for e in range(experts):
            named = (first_ref[0] + e).astype(jnp.float32)
            own = meta[e * seats : (e + 1) * seats]
            gates = pltpu.roll(own, DH - topk, 1)
            rate_ref[e] = jnp.sum(
                jnp.where((own == named) & (lane < topk), gates, 0.0), axis=1, keepdims=True
            )
    tile = 512 if cut % 512 == 0 else cut
    for c in range(0, cut, tile):
        picked[:, c : c + tile] = pick_rows(back_ref, rows, c, tile).astype(jnp.bfloat16)
    for e in range(experts):

        def panel(k, carry, e=e):
            p = e * per_expert + k
            for move in weight_moves(p):
                move.wait()
            w = jnp.concatenate([wg[p], wu[p]], axis=1)
            both = jnp.dot(
                picked[e * seats : (e + 1) * seats], w, preferred_element_type=jnp.float32
            )
            gate, up = both[:, :wide], both[:, wide:]
            if chunk:
                gate, up = gate + gate_in[p], up + up_in[p]
                value = gate / (1.0 + jnp.exp(-gate)) * up * rate_ref[e]
                place = pl.ds(pl.multiple_of(k * wide, wide), wide)
                hidden[e * seats : (e + 1) * seats, place] = value.astype(jnp.bfloat16)
            else:
                gate_ref[p] = gate
                up_ref[p] = up
            return carry

        lax.fori_loop(0, per_expert, panel, 0)
    if chunk == 0:
        for move in early:
            move.wait()
        return
    for p in range(ready, held):
        down_move(p).wait()
    drop_columns(hidden, ready_ref, wd, back_ref, flat, *outs[:2])


def drop_columns(hidden, ready_ref, wd, back_ref, flat, keep_ref, send_ref, first=0):
    cut = flat.shape[1]
    lines = hidden.shape[0]
    ready, wide, _ = ready_ref.shape
    per_expert = hidden.shape[1] // wide
    rest = 0 if wd is None else wd.shape[0] // wide
    experts = (ready + rest) // per_expert
    seats = lines // experts
    tile = 512 if cut % 512 == 0 else cut
    for e in range(experts):
        low, high = e * per_expert, (e + 1) * per_expert
        split = min(max(ready, low), high)
        for c in range(0, cut, tile):
            total = None
            if split > low:
                total = jnp.dot(
                    hidden[e * seats : (e + 1) * seats, : (split - low) * wide],
                    ready_ref[low:split, :, first + c : first + c + tile].reshape(-1, tile),
                    preferred_element_type=jnp.float32,
                )
            if split < high:
                rest = jnp.dot(
                    hidden[e * seats : (e + 1) * seats, (split - low) * wide :],
                    wd[(split - ready) * wide : (high - ready) * wide, c : c + tile],
                    preferred_element_type=jnp.float32,
                )
                total = rest if total is None else total + rest
            flat[e * seats : (e + 1) * seats, c : c + tile] = total.astype(jnp.bfloat16)
    half = keep_ref.shape[0]
    for c in range(0, cut, tile):
        moved = jnp.dot(
            back_ref[...], flat[:, c : c + tile], preferred_element_type=jnp.float32
        ).astype(jnp.bfloat16)
        keep_ref[:, c : c + tile] = moved[:half]
        send_ref[:, c : c + tile] = moved[half:]


def fall_kernel(hidden_ref, ready_ref, back_ref, wd_any, keep_ref, send_ref, flat, *refs):
    ready, wide, depth = ready_ref.shape
    cut = flat.shape[1]
    wd = None
    if refs:
        wd, sem = refs
        moves = [
            pltpu.make_async_copy(
                wd_any.at[p, :, pl.ds(cut, cut)], wd.at[pl.ds((p - ready) * wide, wide)], sem.at[p - ready]
            )
            for p in range(ready, wd_any.shape[0])
        ]
        for move in moves:
            move.start()
        for move in moves:
            move.wait()
    drop_columns(hidden_ref, ready_ref, wd, back_ref, flat, keep_ref, send_ref, first=cut)


def fall_call(hidden, ready, back, w_down):
    held, wide, depth = w_down.shape
    rest = held - ready.shape[0]
    cut = depth // 2
    full = pl.BlockSpec(memory_space=pltpu.VMEM)
    shape = jax.ShapeDtypeStruct((back.shape[0] // 2, cut), jnp.bfloat16)
    scratch = [pltpu.VMEM((hidden.shape[0], cut), jnp.bfloat16)]
    if rest:
        scratch += [pltpu.VMEM((rest * wide, cut), jnp.bfloat16), pltpu.SemaphoreType.DMA((rest,))]
    return pl.pallas_call(
        fall_kernel,
        out_shape=(shape, shape),
        in_specs=[full, full, full, pl.BlockSpec(memory_space=pltpu.HBM)],
        out_specs=(full, full),
        scratch_shapes=scratch,
        compiler_params=pltpu.CompilerParams(vmem_limit_bytes=LAST_LIMIT),
        cost_estimate=pl.CostEstimate(
            flops=2 * held * hidden.shape[0] * cut * wide + 2 * hidden.shape[0] * back.shape[0] * cut,
            bytes_accessed=2 * rest * cut * wide,
            transcendentals=0,
        ),
    )(hidden, ready, back, w_down)


def expert_call(rows, w_gate, w_up, chunk, cut, topk, experts, seats, first=None, sums=None, w_down=None):
    held, depth, wide = w_gate.shape
    count = rows[0].shape[0] * len(rows)
    full = pl.BlockSpec(memory_space=pltpu.VMEM)
    anywhere = pl.BlockSpec(memory_space=pl.ANY)
    far = pl.BlockSpec(memory_space=pltpu.HBM)
    deep = held // experts * wide
    args = [*rows, w_gate, w_up]
    in_specs = [anywhere] * len(rows) + [far, far]
    scratch = [
        pltpu.VMEM((count, rows[0].shape[1]), jnp.bfloat16),
        pltpu.VMEM((experts * seats, cut), jnp.bfloat16),
        pltpu.VMEM((held, cut, wide), jnp.bfloat16),
        pltpu.VMEM((held, cut, wide), jnp.bfloat16),
        pltpu.SemaphoreType.DMA((len(rows),)),
        pltpu.SemaphoreType.DMA((held,)),
        pltpu.SemaphoreType.DMA((held,)),
    ]
    flops = 4 * held * seats * cut * wide + 2 * experts * seats * count * cut
    moved = 4 * held * cut * wide + 2 * count * cut
    if chunk == 0:
        early = max(1, held * READY // 16)
        args += [first, w_down]
        in_specs += [pl.BlockSpec(memory_space=pltpu.SMEM), far]
        outs = [jax.ShapeDtypeStruct((held, seats, wide), jnp.float32)] * 2 + [
            jax.ShapeDtypeStruct((count, experts * seats), jnp.bfloat16),
            jax.ShapeDtypeStruct((experts, seats, 1), jnp.float32),
            jax.ShapeDtypeStruct((early, wide, depth), jnp.bfloat16),
        ]
        scratch += [pltpu.SemaphoreType.DMA((early,))]
        moved += 2 * early * wide * depth
    else:
        ready = sums[4]
        args += [*sums, w_down]
        in_specs += [full] * 5 + [far]
        outs = [jax.ShapeDtypeStruct((count // 2, cut), jnp.bfloat16)] * 2
        outs += [jax.ShapeDtypeStruct((experts * seats, deep), jnp.bfloat16)]
        scratch += [
            pltpu.VMEM(((held - ready.shape[0]) * wide or 8, cut), jnp.bfloat16),
            pltpu.VMEM((experts * seats, cut), jnp.bfloat16),
            pltpu.SemaphoreType.DMA((max(1, held - ready.shape[0]),)),
        ]
        flops += 2 * held * seats * cut * wide + 2 * experts * seats * count * cut
        moved += held * depth * wide
    return pl.pallas_call(
        functools.partial(expert_kernel, len(rows), experts, seats, topk, chunk),
        out_shape=tuple(outs),
        in_specs=in_specs,
        out_specs=tuple([full] * len(outs)),
        scratch_shapes=scratch,
        compiler_params=pltpu.CompilerParams(vmem_limit_bytes=RISE_LIMIT if chunk == 0 else FALL_LIMIT),
        cost_estimate=pl.CostEstimate(
            flops=flops, bytes_accessed=moved, transcendentals=0
        ),
    )(*args)


def body(
    queries,
    kv_cache,
    tree_kv,
    context_lengths,
    tree_parents,
    resid,
    out_weight,
    norm_gain,
    expert_ids,
    gate_weights,
    w_gate,
    w_up,
    w_down,
):
    here = lax.axis_index("seq")
    there = lax.axis_index("req")
    parts = lax.axis_size("seq")
    groups = lax.axis_size("req")
    bits = parts.bit_length() - 1
    order = block_order(parts)
    near = order[: parts // 2]
    own = queries.shape[1]
    rows = own * parts
    depth = resid.shape[2]

    span = kv_cache.shape[1]
    share = parts // KVH
    lane = kv_cache[0]
    heads = [
        lane[:, :, h * DH : (h + 1) * DH].reshape(span, 2 * DH) for h in range(KVH)
    ]

    def head_of(device):
        pick = heads[0]
        for h in range(1, KVH):
            pick = jnp.where(device // share == h, heads[h], pick)
        return pick

    same, other = head_of(here), head_of(here ^ (parts // 2))
    turns = [near[0]] + ([near[i] for i in (2, 3, 1)] if len(near) == 4 else near[1:])
    order_kv = turns + [mask ^ 1 for mask in turns]
    half = [same] + [hop(other if mask & (parts // 2) else same, mask) for mask in turns[1:]]
    valid = context_lengths[0] - jnp.stack([(here ^ mask) * span for mask in order_kv])

    mine = HQ // parts
    tree_heads = [
        tree_kv[0][:, :, h * DH : (h + 1) * DH].reshape(own, 2 * DH) for h in range(KVH)
    ]
    asked = jnp.transpose(queries[0].reshape(own, parts, mine * DH), (1, 0, 2))
    trees = jnp.stack(tree_heads)[:, None]
    trees = jnp.broadcast_to(trees, (KVH, share, own, 2 * DH)).reshape(parts, own, 2 * DH)
    packed = jnp.concatenate([asked, trees], axis=2)
    packed = lax.all_to_all(packed, "seq", split_axis=0, concat_axis=0, tiled=True)
    packed = packed.reshape(rows, -1)

    wanted = jnp.stack([here ^ mask for mask in order])
    wanted = (wanted[:, None] * own + jnp.arange(own, dtype=jnp.int32)[None, :]).reshape(rows)
    perm = (wanted[:, None] == jnp.arange(rows, dtype=jnp.int32)[None, :]).astype(jnp.bfloat16)

    linked = ancestry(tree_parents[0])
    blocks = half + [hop(piece, 1) for piece in half]
    keep, send = attend(valid.astype(jnp.int32), perm, packed, linked, blocks, out_weight)

    got = hop(send, 1)
    pair = [
        keep[i * own : (i + 1) * own].astype(jnp.float32)
        + got[i * own : (i + 1) * own].astype(jnp.float32)
        for i in range(len(near))
    ]
    terms = [pair[0]] + [
        hop(pair[i].astype(jnp.bfloat16), near[i]).astype(jnp.float32)
        for i in range(1, len(near))
    ]
    attended = sum(terms[1:], terms[0]).astype(jnp.bfloat16)
    mid = (resid[0].astype(jnp.float32) + attended.astype(jnp.float32)).astype(jnp.bfloat16)
    midf = lax.optimization_barrier(mid).astype(jnp.float32)
    factor = lax.rsqrt(jnp.mean(midf * midf, axis=-1, keepdims=True) + EPS)
    normed = (midf * factor * norm_gain.astype(jnp.float32)).astype(jnp.bfloat16)

    table = jnp.concatenate(
        [expert_ids[0].astype(jnp.bfloat16), gate_weights[0]], axis=1
    )
    table = lax.dynamic_slice_in_dim(table, here * own, own, 0)
    topk = expert_ids.shape[2]
    table = jnp.pad(table, ((0, 0), (0, DH - 2 * topk)))
    held = w_gate.shape[0]
    experts = max(1, held // SPLIT)
    first = (((there * parts + here) * held) // SPLIT).astype(jnp.int32).reshape(1)
    seats = groups * CAP

    cut = depth // 2
    ring = [near[0]] + ([near[i] for i in (3, 1, 2)] if len(near) == 4 else near[1:])
    planes = []
    for chunk in range(2):
        piece = normed[:, chunk * cut : (chunk + 1) * cut]
        if chunk == 0:
            piece = jnp.concatenate([piece, table], axis=1)
        stack = jnp.concatenate([piece] + [turn(piece, d) for d in range(1, groups)], axis=0)
        planes.append([stack] + [hop(stack, mask) for mask in ring[1:]])
    full = planes[0] + [hop(p, 1) for p in planes[0]]
    sums = expert_call(full, w_gate, w_up, 0, cut, topk, experts, seats, first=first, w_down=w_down)
    *plane, gate = lax.optimization_barrier((*planes[1], sums[0]))
    full = plane + [hop(p, 1) for p in plane]
    keep0, send0, hidden = expert_call(
        full, w_gate, w_up, 1, cut, topk, experts, seats, sums=(gate, *sums[1:]), w_down=w_down
    )

    size = groups * own

    def paired(keep, got):
        return {
            mask: keep[i * size : (i + 1) * size].astype(jnp.float32)
            + got[i * size : (i + 1) * size].astype(jnp.float32)
            for i, mask in enumerate(ring)
        }

    def send(value, mask):
        return hop(value.astype(jnp.bfloat16), mask).astype(jnp.float32)

    def home(flat):
        result = flat[:own]
        for d in range(1, groups):
            result = result + turn(
                flat[d * own : (d + 1) * own].astype(jnp.bfloat16), d
            ).astype(jnp.float32)
        return result.astype(jnp.bfloat16)

    got0 = hop(send0, 1)
    keep1, send1 = fall_call(hidden, sums[4], sums[2], w_down)
    send1, got0 = lax.optimization_barrier((send1, got0))
    got1 = hop(send1, 1)
    low, high = paired(keep0, got0), paired(keep1, got1)
    if len(near) == 4:
        near_x, near_y = 2, 4
        far = near_x ^ near_y
        got_low, got_high = send(low[far], near_x), send(high[far], near_y)
        go_x, go_y = low[near_x].astype(jnp.bfloat16), (low[near_y] + got_low).astype(jnp.bfloat16)
        go_x, go_y, got_high = lax.optimization_barrier((go_x, go_y, got_high))
        got_x, got_y = send(go_x, near_x), send(go_y, near_y)
        flat_low = low[0] + got_x + got_y
        go_x, go_y = (high[near_x] + got_high).astype(jnp.bfloat16), high[near_y].astype(jnp.bfloat16)
        go_x, go_y, flat_low = lax.optimization_barrier((go_x, go_y, flat_low))
        flat_high = high[0] + send(go_x, near_x) + send(go_y, near_y)
    else:
        flat_low, flat_high = (
            sum([send(blocks[mask], mask) for mask in near[1:]], blocks[0]) for blocks in (low, high)
        )
    pieces = [home(flat_low), home(flat_high)]
    return (attended[None], jnp.concatenate(pieces, axis=1)[None])


def solution(mesh):
    placed = (
        P("req", "seq", None),
        P("req", "seq", None, None),
        P("req", "seq", None, None),
        P("req"),
        P("req", None),
        P("req", "seq", None),
        P("seq", None),
        P(),
        P("req", None, None),
        P("req", None, None),
        P(("req", "seq"), None, None),
        P(("req", "seq"), None, None),
        P(("req", "seq"), None, None),
    )
    return jax.shard_map(
        body,
        mesh=mesh,
        in_specs=placed,
        out_specs=(P("req", "seq", None), P("req", "seq", None)),
        check_vma=False,
    )
```

```python
import functools

import jax
import jax.numpy as jnp
from jax import lax
from jax.experimental import pallas as pl
from jax.experimental.pallas import tpu as pltpu
from jax.sharding import PartitionSpec as P

DH = 128
HQ = 32
KVH = 2
EXPERTS = 64
CAP = 32
SPLIT = 8


NEG = -1e30
EPS = 1e-06
RISE_LIMIT = 30 * 1024 * 1024
FALL_LIMIT = 29 * 1024 * 1024
LAST_LIMIT = 26 * 1024 * 1024
ATTEND_LIMIT = 48 * 1024 * 1024
READY = 12
LOG2E = 1.4426950408889634


def hop(value, mask):
    count = lax.axis_size("seq")
    return lax.ppermute(value, "seq", [(i, i ^ mask) for i in range(count)])


def turn(value, step):
    count = lax.axis_size("req")
    return lax.ppermute(value, "req", [(i, i ^ step) for i in range(count)])


def block_order(parts):
    bits = parts.bit_length() - 1
    return [int(format(p, "b").zfill(bits)[::-1], 2) if bits else 0 for p in range(parts)]


def ancestry(parents):
    count = parents.shape[0]
    node = jnp.arange(count, dtype=jnp.int32)
    linked = (parents[:, None] == node[None, :]) | (node[:, None] == node[None, :])
    reach = linked.astype(jnp.bfloat16)
    hops = 1
    while hops < count:
        paths = jnp.dot(reach, reach, preferred_element_type=jnp.float32)
        reach = jnp.minimum(paths, 1.0).astype(jnp.bfloat16)
        hops = hops * 2
    return reach


def weigh(weights, values):
    values = jnp.concatenate([values, jnp.ones_like(values)], axis=1)
    return jnp.dot(weights.astype(jnp.bfloat16), values, preferred_element_type=jnp.float32)


def attend_kernel(parts, mine, valid_ref, perm_ref, packed_ref, mask_ref, *refs):
    kv_refs = refs[:parts]
    w_any, keep_ref, send_ref, w_ref, sem = refs[parts:]
    copy = pltpu.make_async_copy(w_any, w_ref, sem)
    copy.start()
    rows = packed_ref.shape[0]
    lanes = mine * DH
    scale = DH ** (-0.5) * LOG2E
    perm = perm_ref[...]
    q = jnp.dot(perm, packed_ref[:, :lanes], preferred_element_type=jnp.float32).astype(jnp.bfloat16)
    q = jnp.concatenate([q[:, a * DH : (a + 1) * DH] for a in range(mine)], axis=0)

    def scores(keys):
        return (
            lax.dot_general(q, keys, (((1,), (1,)), ((), ())), preferred_element_type=jnp.float32)
            * scale
        )

    mask = jnp.dot(perm, mask_ref[...], preferred_element_type=jnp.float32)
    linked = jnp.concatenate([mask] * mine, axis=0) > 0.5
    s = jnp.where(linked, scores(packed_ref[:, lanes : lanes + DH]), NEG)
    top = jnp.max(s, axis=-1, keepdims=True)
    out = weigh(jnp.exp2(s - top), packed_ref[:, lanes + DH :])
    for part in range(parts):
        kv = kv_refs[part]
        place = lax.broadcasted_iota(jnp.int32, (1, kv.shape[0]), 1)
        bias = jnp.where(place < valid_ref[part], 0.0, NEG)
        s = scores(kv[:, :DH]) + bias
        peak = jnp.maximum(top, jnp.max(s, axis=-1, keepdims=True))
        out = out * jnp.exp2(top - peak) + weigh(jnp.exp2(s - peak), kv[:, DH:])
        top = peak
    attention = (out[:, :DH] / out[:, DH:]).astype(jnp.bfloat16)
    attention = jnp.concatenate(
        [attention[a * rows : (a + 1) * rows] for a in range(mine)], axis=1
    )
    copy.wait()
    half = rows // 2
    width = w_ref.shape[1]
    tile = min(width, 1024)
    for first in range(0, width, tile):
        piece = jnp.dot(
            attention, w_ref[:, first : first + tile], preferred_element_type=jnp.float32
        ).astype(jnp.bfloat16)
        keep_ref[:, first : first + tile] = piece[:half]
        send_ref[:, first : first + tile] = piece[half:]


def attend(valid, perm, packed, mask, blocks, w):
    parts = len(blocks)
    rows, mine = packed.shape[0], (packed.shape[1] - 2 * DH) // DH
    span = blocks[0].shape[0]
    full = pl.BlockSpec(memory_space=pltpu.VMEM)
    out = jax.ShapeDtypeStruct((rows // 2, w.shape[1]), jnp.bfloat16)
    reach = rows + parts * span
    return pl.pallas_call(
        functools.partial(attend_kernel, parts, mine),
        out_shape=(out, out),
        in_specs=[pl.BlockSpec(memory_space=pltpu.SMEM)]
        + [full] * (parts + 3)
        + [pl.BlockSpec(memory_space=pltpu.HBM)],
        out_specs=(full, full),
        scratch_shapes=[pltpu.VMEM(w.shape, w.dtype), pltpu.SemaphoreType.DMA],
        compiler_params=pltpu.CompilerParams(vmem_limit_bytes=ATTEND_LIMIT),
        cost_estimate=pl.CostEstimate(
            flops=4 * rows * mine * DH * reach + 2 * rows * mine * DH * w.shape[1],
            bytes_accessed=2 * w.size + 4 * DH * reach + 2 * rows * w.shape[1],
            transcendentals=rows * mine * reach,
        ),
    )(valid, perm, packed, mask, *blocks, w)


def seat_rows(first_ref, topk, table, back_ref, experts, seats):
    count = table.shape[0]
    block = min(count, 256)
    lane = lax.broadcasted_iota(jnp.int32, (count, DH), 1)
    hits = []
    spread = jnp.zeros((count, DH), jnp.float32)
    for e in range(experts):
        named = (first_ref[0] + e).astype(jnp.float32)
        match = jnp.where((table == named) & (lane < topk), 1.0, 0.0)
        hits.append(jnp.max(match, axis=1, keepdims=True))
        spread = spread + jnp.where(lane == e, hits[e], 0.0)
    ahead = lax.broadcasted_iota(jnp.int32, (block, block), 0) > lax.broadcasted_iota(
        jnp.int32, (block, block), 1
    )
    ahead = jnp.where(ahead, 1.0, 0.0).astype(jnp.bfloat16)
    place = lax.broadcasted_iota(jnp.int32, (block, seats), 1).astype(jnp.float32)
    carry = jnp.zeros((1, DH), jnp.float32)
    for at in range(0, count, block):
        here = spread[at : at + block]
        before = carry + jnp.dot(
            ahead, here.astype(jnp.bfloat16), preferred_element_type=jnp.float32
        )
        carry = carry + jnp.sum(here, axis=0, keepdims=True)
        for e in range(experts):
            seat = jnp.sum(jnp.where(lane[:block] == e, before, 0.0), axis=1, keepdims=True)
            taken = (hits[e][at : at + block] > 0.5) & (seat == place)
            back_ref[at : at + block, e * seats : (e + 1) * seats] = jnp.where(
                taken, 1.0, 0.0
            ).astype(jnp.bfloat16)


def pick_rows(back_ref, rows, first, width):
    return lax.dot_general(
        back_ref[...],
        rows[:, first : first + width],
        (((0,), (0,)), ((), ())),
        preferred_element_type=jnp.float32,
    )


def expert_kernel(pieces, experts, seats, topk, chunk, *refs):
    refs = list(refs)

    def take(count):
        out = refs[:count]
        del refs[:count]
        return out

    part_refs = take(pieces)
    wg_any, wu_any = take(2)
    if chunk == 0:
        first_ref, wd_any = take(2)
        gate_ref, up_ref, back_ref, rate_ref, ready_ref = take(5)
    else:
        gate_in, up_in, back_ref, rate_ref, ready_ref, wd_any = take(6)
        outs = take(3)
        hidden = outs[2]
    rows, picked, wg, wu, part_sem, gate_sem, up_sem = take(7)
    held, cut, wide = wg.shape
    per_expert = held // experts
    size = rows.shape[0] // pieces
    moves = [
        pltpu.make_async_copy(ref, rows.at[pl.ds(i * size, size)], part_sem.at[i])
        for i, ref in enumerate(part_refs)
    ]
    for move in moves:
        move.start()
    first = chunk * cut

    def weight_moves(p):
        return (
            pltpu.make_async_copy(wg_any.at[p, pl.ds(first, cut)], wg.at[p], gate_sem.at[p]),
            pltpu.make_async_copy(wu_any.at[p, pl.ds(first, cut)], wu.at[p], up_sem.at[p]),
        )

    for p in range(held):
        for move in weight_moves(p):
            move.start()
    if chunk == 0:
        (ready_sem,) = take(1)
        early = [
            pltpu.make_async_copy(wd_any.at[p], ready_ref.at[p], ready_sem.at[p])
            for p in range(ready_ref.shape[0])
        ]
        for move in early:
            move.start()
    else:
        wd, flat, down_sem = take(3)

        ready = ready_ref.shape[0]

        def down_move(p):
            place = pl.ds((p - ready) * wide, wide)
            return pltpu.make_async_copy(
                wd_any.at[p, :, pl.ds(0, cut)], wd.at[place], down_sem.at[p - ready]
            )

        for p in range(ready, held):
            down_move(p).start()
    for move in moves:
        move.wait()
    if chunk == 0:
        seat_rows(first_ref, topk, rows[:, cut:].astype(jnp.float32), back_ref, experts, seats)
        meta = pick_rows(back_ref, rows, cut, DH)
        lane = lax.broadcasted_iota(jnp.int32, (seats, DH), 1)
        for e in range(experts):
            named = (first_ref[0] + e).astype(jnp.float32)
            own = meta[e * seats : (e + 1) * seats]
            gates = pltpu.roll(own, DH - topk, 1)
            rate_ref[e] = jnp.sum(
                jnp.where((own == named) & (lane < topk), gates, 0.0), axis=1, keepdims=True
            )
    tile = 512 if cut % 512 == 0 else cut
    for c in range(0, cut, tile):
        picked[:, c : c + tile] = pick_rows(back_ref, rows, c, tile).astype(jnp.bfloat16)
    for e in range(experts):

        def panel(k, carry, e=e):
            p = e * per_expert + k
            for move in weight_moves(p):
                move.wait()
            w = jnp.concatenate([wg[p], wu[p]], axis=1)
            both = jnp.dot(
                picked[e * seats : (e + 1) * seats], w, preferred_element_type=jnp.float32
            )
            gate, up = both[:, :wide], both[:, wide:]
            if chunk:
                gate, up = gate + gate_in[p], up + up_in[p]
                value = gate / (1.0 + jnp.exp(-gate)) * up * rate_ref[e]
                place = pl.ds(pl.multiple_of(k * wide, wide), wide)
                hidden[e * seats : (e + 1) * seats, place] = value.astype(jnp.bfloat16)
            else:
                gate_ref[p] = gate
                up_ref[p] = up
            return carry

        lax.fori_loop(0, per_expert, panel, 0)
    if chunk == 0:
        for move in early:
            move.wait()
        return
    moves = [down_move(p) for p in range(ready, held)]
    drop_columns(hidden, ready_ref, wd, back_ref, flat, *outs[:2], moves)


def drop_columns(hidden, ready_ref, wd, back_ref, flat, keep_ref, send_ref, moves, first=0):
    cut = flat.shape[1]
    lines = hidden.shape[0]
    ready, wide, _ = ready_ref.shape
    per_expert = hidden.shape[1] // wide
    rest = 0 if wd is None else wd.shape[0] // wide
    experts = (ready + rest) // per_expert
    seats = lines // experts
    tile = 512 if cut % 512 == 0 else cut
    for e in range(experts):
        low, high = e * per_expert, (e + 1) * per_expert
        split = min(max(ready, low), high)
        for move in moves[split - ready : high - ready] if split < high else []:
            move.wait()
        for c in range(0, cut, tile):
            total = None
            if split > low:
                total = jnp.dot(
                    hidden[e * seats : (e + 1) * seats, : (split - low) * wide],
                    ready_ref[low:split, :, first + c : first + c + tile].reshape(-1, tile),
                    preferred_element_type=jnp.float32,
                )
            if split < high:
                rest = jnp.dot(
                    hidden[e * seats : (e + 1) * seats, (split - low) * wide :],
                    wd[(split - ready) * wide : (high - ready) * wide, c : c + tile],
                    preferred_element_type=jnp.float32,
                )
                total = rest if total is None else total + rest
            flat[e * seats : (e + 1) * seats, c : c + tile] = total.astype(jnp.bfloat16)
    half = keep_ref.shape[0]
    for c in range(0, cut, tile):
        moved = jnp.dot(
            back_ref[...], flat[:, c : c + tile], preferred_element_type=jnp.float32
        ).astype(jnp.bfloat16)
        keep_ref[:, c : c + tile] = moved[:half]
        send_ref[:, c : c + tile] = moved[half:]


def fall_kernel(hidden_ref, ready_ref, back_ref, wd_any, keep_ref, send_ref, flat, *refs):
    ready, wide, depth = ready_ref.shape
    cut = flat.shape[1]
    wd, moves = None, []
    if refs:
        wd, sem = refs
        moves = [
            pltpu.make_async_copy(
                wd_any.at[p, :, pl.ds(cut, cut)], wd.at[pl.ds((p - ready) * wide, wide)], sem.at[p - ready]
            )
            for p in range(ready, wd_any.shape[0])
        ]
        for move in moves:
            move.start()
    drop_columns(hidden_ref, ready_ref, wd, back_ref, flat, keep_ref, send_ref, moves, first=cut)


def fall_call(hidden, ready, back, w_down):
    held, wide, depth = w_down.shape
    rest = held - ready.shape[0]
    cut = depth // 2
    full = pl.BlockSpec(memory_space=pltpu.VMEM)
    shape = jax.ShapeDtypeStruct((back.shape[0] // 2, cut), jnp.bfloat16)
    scratch = [pltpu.VMEM((hidden.shape[0], cut), jnp.bfloat16)]
    if rest:
        scratch += [pltpu.VMEM((rest * wide, cut), jnp.bfloat16), pltpu.SemaphoreType.DMA((rest,))]
    return pl.pallas_call(
        fall_kernel,
        out_shape=(shape, shape),
        in_specs=[full, full, full, pl.BlockSpec(memory_space=pltpu.HBM)],
        out_specs=(full, full),
        scratch_shapes=scratch,
        compiler_params=pltpu.CompilerParams(vmem_limit_bytes=LAST_LIMIT),
        cost_estimate=pl.CostEstimate(
            flops=2 * held * hidden.shape[0] * cut * wide + 2 * hidden.shape[0] * back.shape[0] * cut,
            bytes_accessed=2 * rest * cut * wide,
            transcendentals=0,
        ),
    )(hidden, ready, back, w_down)


def expert_call(rows, w_gate, w_up, chunk, cut, topk, experts, seats, first=None, sums=None, w_down=None):
    held, depth, wide = w_gate.shape
    count = rows[0].shape[0] * len(rows)
    full = pl.BlockSpec(memory_space=pltpu.VMEM)
    anywhere = pl.BlockSpec(memory_space=pl.ANY)
    far = pl.BlockSpec(memory_space=pltpu.HBM)
    deep = held // experts * wide
    args = [*rows, w_gate, w_up]
    in_specs = [anywhere] * len(rows) + [far, far]
    scratch = [
        pltpu.VMEM((count, rows[0].shape[1]), jnp.bfloat16),
        pltpu.VMEM((experts * seats, cut), jnp.bfloat16),
        pltpu.VMEM((held, cut, wide), jnp.bfloat16),
        pltpu.VMEM((held, cut, wide), jnp.bfloat16),
        pltpu.SemaphoreType.DMA((len(rows),)),
        pltpu.SemaphoreType.DMA((held,)),
        pltpu.SemaphoreType.DMA((held,)),
    ]
    flops = 4 * held * seats * cut * wide + 2 * experts * seats * count * cut
    moved = 4 * held * cut * wide + 2 * count * cut
    if chunk == 0:
        early = max(1, held * READY // 16)
        args += [first, w_down]
        in_specs += [pl.BlockSpec(memory_space=pltpu.SMEM), far]
        outs = [jax.ShapeDtypeStruct((held, seats, wide), jnp.float32)] * 2 + [
            jax.ShapeDtypeStruct((count, experts * seats), jnp.bfloat16),
            jax.ShapeDtypeStruct((experts, seats, 1), jnp.float32),
            jax.ShapeDtypeStruct((early, wide, depth), jnp.bfloat16),
        ]
        scratch += [pltpu.SemaphoreType.DMA((early,))]
        moved += 2 * early * wide * depth
    else:
        ready = sums[4]
        args += [*sums, w_down]
        in_specs += [full] * 5 + [far]
        outs = [jax.ShapeDtypeStruct((count // 2, cut), jnp.bfloat16)] * 2
        outs += [jax.ShapeDtypeStruct((experts * seats, deep), jnp.bfloat16)]
        scratch += [
            pltpu.VMEM(((held - ready.shape[0]) * wide or 8, cut), jnp.bfloat16),
            pltpu.VMEM((experts * seats, cut), jnp.bfloat16),
            pltpu.SemaphoreType.DMA((max(1, held - ready.shape[0]),)),
        ]
        flops += 2 * held * seats * cut * wide + 2 * experts * seats * count * cut
        moved += held * depth * wide
    return pl.pallas_call(
        functools.partial(expert_kernel, len(rows), experts, seats, topk, chunk),
        out_shape=tuple(outs),
        in_specs=in_specs,
        out_specs=tuple([full] * len(outs)),
        scratch_shapes=scratch,
        compiler_params=pltpu.CompilerParams(vmem_limit_bytes=RISE_LIMIT if chunk == 0 else FALL_LIMIT),
        cost_estimate=pl.CostEstimate(
            flops=flops, bytes_accessed=moved, transcendentals=0
        ),
    )(*args)


def body(
    queries,
    kv_cache,
    tree_kv,
    context_lengths,
    tree_parents,
    resid,
    out_weight,
    norm_gain,
    expert_ids,
    gate_weights,
    w_gate,
    w_up,
    w_down,
):
    here = lax.axis_index("seq")
    there = lax.axis_index("req")
    parts = lax.axis_size("seq")
    groups = lax.axis_size("req")
    bits = parts.bit_length() - 1
    order = block_order(parts)
    near = order[: parts // 2]
    own = queries.shape[1]
    rows = own * parts
    depth = resid.shape[2]

    span = kv_cache.shape[1]
    share = parts // KVH
    lane = kv_cache[0]
    heads = [
        lane[:, :, h * DH : (h + 1) * DH].reshape(span, 2 * DH) for h in range(KVH)
    ]

    def head_of(device):
        pick = heads[0]
        for h in range(1, KVH):
            pick = jnp.where(device // share == h, heads[h], pick)
        return pick

    same, other = head_of(here), head_of(here ^ (parts // 2))
    turns = [near[0]] + ([near[i] for i in (2, 3, 1)] if len(near) == 4 else near[1:])
    order_kv = turns + [mask ^ 1 for mask in turns]
    half = [same] + [hop(other if mask & (parts // 2) else same, mask) for mask in turns[1:]]
    valid = context_lengths[0] - jnp.stack([(here ^ mask) * span for mask in order_kv])

    mine = HQ // parts
    tree_heads = [
        tree_kv[0][:, :, h * DH : (h + 1) * DH].reshape(own, 2 * DH) for h in range(KVH)
    ]
    asked = jnp.transpose(queries[0].reshape(own, parts, mine * DH), (1, 0, 2))
    trees = jnp.stack(tree_heads)[:, None]
    trees = jnp.broadcast_to(trees, (KVH, share, own, 2 * DH)).reshape(parts, own, 2 * DH)
    packed = jnp.concatenate([asked, trees], axis=2)
    packed = lax.all_to_all(packed, "seq", split_axis=0, concat_axis=0, tiled=True)
    packed = packed.reshape(rows, -1)

    wanted = jnp.stack([here ^ mask for mask in order])
    wanted = (wanted[:, None] * own + jnp.arange(own, dtype=jnp.int32)[None, :]).reshape(rows)
    perm = (wanted[:, None] == jnp.arange(rows, dtype=jnp.int32)[None, :]).astype(jnp.bfloat16)

    linked = ancestry(tree_parents[0])
    blocks = half + [hop(piece, 1) for piece in half]
    keep, send = attend(valid.astype(jnp.int32), perm, packed, linked, blocks, out_weight)

    got = hop(send, 1)
    pair = [
        keep[i * own : (i + 1) * own].astype(jnp.float32)
        + got[i * own : (i + 1) * own].astype(jnp.float32)
        for i in range(len(near))
    ]
    terms = [pair[0]] + [
        hop(pair[i].astype(jnp.bfloat16), near[i]).astype(jnp.float32)
        for i in range(1, len(near))
    ]
    attended = sum(terms[1:], terms[0]).astype(jnp.bfloat16)
    mid = (resid[0].astype(jnp.float32) + attended.astype(jnp.float32)).astype(jnp.bfloat16)
    midf = lax.optimization_barrier(mid).astype(jnp.float32)
    factor = lax.rsqrt(jnp.mean(midf * midf, axis=-1, keepdims=True) + EPS)
    normed = (midf * factor * norm_gain.astype(jnp.float32)).astype(jnp.bfloat16)

    table = jnp.concatenate(
        [expert_ids[0].astype(jnp.bfloat16), gate_weights[0]], axis=1
    )
    table = lax.dynamic_slice_in_dim(table, here * own, own, 0)
    topk = expert_ids.shape[2]
    table = jnp.pad(table, ((0, 0), (0, DH - 2 * topk)))
    held = w_gate.shape[0]
    experts = max(1, held // SPLIT)
    first = (((there * parts + here) * held) // SPLIT).astype(jnp.int32).reshape(1)
    seats = groups * CAP

    cut = depth // 2
    ring = [near[0]] + ([near[i] for i in (3, 1, 2)] if len(near) == 4 else near[1:])
    planes = []
    for chunk in range(2):
        piece = normed[:, chunk * cut : (chunk + 1) * cut]
        if chunk == 0:
            piece = jnp.concatenate([piece, table], axis=1)
        stack = jnp.concatenate([piece] + [turn(piece, d) for d in range(1, groups)], axis=0)
        planes.append([stack] + [hop(stack, mask) for mask in ring[1:]])
    full = planes[0] + [hop(p, 1) for p in planes[0]]
    sums = expert_call(full, w_gate, w_up, 0, cut, topk, experts, seats, first=first, w_down=w_down)
    plane = planes[1][:1]
    gate = sums[0]
    for piece in planes[1][1:]:
        plane.append(lax.optimization_barrier((piece, gate))[0])
    full = plane + [hop(p, 1) for p in plane]
    keep0, send0, hidden = expert_call(
        full, w_gate, w_up, 1, cut, topk, experts, seats, sums=(gate, *sums[1:]), w_down=w_down
    )

    size = groups * own

    def paired(keep, got):
        return {
            mask: keep[i * size : (i + 1) * size].astype(jnp.float32)
            + got[i * size : (i + 1) * size].astype(jnp.float32)
            for i, mask in enumerate(ring)
        }

    def send(value, mask):
        return hop(value.astype(jnp.bfloat16), mask).astype(jnp.float32)

    def home(flat):
        result = flat[:own]
        for d in range(1, groups):
            result = result + turn(
                flat[d * own : (d + 1) * own].astype(jnp.bfloat16), d
            ).astype(jnp.float32)
        return result.astype(jnp.bfloat16)

    got0 = hop(send0, 1)
    keep1, send1 = fall_call(hidden, sums[4], sums[2], w_down)
    send1, got0 = lax.optimization_barrier((send1, got0))
    got1 = hop(send1, 1)
    low, high = paired(keep0, got0), paired(keep1, got1)
    if len(near) == 4:
        near_x, near_y = 2, 4
        far = near_x ^ near_y
        got_low, got_high = send(low[far], near_x), send(high[far], near_y)
        go_x, go_y = low[near_x].astype(jnp.bfloat16), (low[near_y] + got_low).astype(jnp.bfloat16)
        go_x, go_y, got_high = lax.optimization_barrier((go_x, go_y, got_high))
        got_x, got_y = send(go_x, near_x), send(go_y, near_y)
        flat_low = low[0] + got_x + got_y
        go_x, go_y = (high[near_x] + got_high).astype(jnp.bfloat16), high[near_y].astype(jnp.bfloat16)
        go_x, go_y, flat_low = lax.optimization_barrier((go_x, go_y, flat_low))
        flat_high = high[0] + send(go_x, near_x) + send(go_y, near_y)
    else:
        flat_low, flat_high = (
            sum([send(blocks[mask], mask) for mask in near[1:]], blocks[0]) for blocks in (low, high)
        )
    pieces = [home(flat_low), home(flat_high)]
    return (attended[None], jnp.concatenate(pieces, axis=1)[None])


def solution(mesh):
    placed = (
        P("req", "seq", None),
        P("req", "seq", None, None),
        P("req", "seq", None, None),
        P("req"),
        P("req", None),
        P("req", "seq", None),
        P("seq", None),
        P(),
        P("req", None, None),
        P("req", None, None),
        P(("req", "seq"), None, None),
        P(("req", "seq"), None, None),
        P(("req", "seq"), None, None),
    )
    return jax.shard_map(
        body,
        mesh=mesh,
        in_specs=placed,
        out_specs=(P("req", "seq", None), P("req", "seq", None)),
        check_vma=False,
    )
```

```python
import functools

import jax
import jax.numpy as jnp
from jax import lax
from jax.experimental import pallas as pl
from jax.experimental.pallas import tpu as pltpu
from jax.sharding import PartitionSpec as P

DH = 128
HQ = 32
KVH = 2
EXPERTS = 64
CAP = 32
SPLIT = 8


NEG = -1e30
EPS = 1e-06
RISE_LIMIT = 30 * 1024 * 1024
FALL_LIMIT = 29 * 1024 * 1024
LAST_LIMIT = 26 * 1024 * 1024
ATTEND_LIMIT = 48 * 1024 * 1024
READY = 12
LOG2E = 1.4426950408889634


def hop(value, mask):
    count = lax.axis_size("seq")
    return lax.ppermute(value, "seq", [(i, i ^ mask) for i in range(count)])


def turn(value, step):
    count = lax.axis_size("req")
    return lax.ppermute(value, "req", [(i, i ^ step) for i in range(count)])


def block_order(parts):
    bits = parts.bit_length() - 1
    return [int(format(p, "b").zfill(bits)[::-1], 2) if bits else 0 for p in range(parts)]


def ancestry(parents):
    count = parents.shape[0]
    node = jnp.arange(count, dtype=jnp.int32)
    linked = (parents[:, None] == node[None, :]) | (node[:, None] == node[None, :])
    reach = linked.astype(jnp.bfloat16)
    hops = 1
    while hops < count:
        paths = jnp.dot(reach, reach, preferred_element_type=jnp.float32)
        reach = jnp.minimum(paths, 1.0).astype(jnp.bfloat16)
        hops = hops * 2
    return reach


def weigh(weights, values):
    values = jnp.concatenate([values, jnp.ones_like(values)], axis=1)
    return jnp.dot(weights.astype(jnp.bfloat16), values, preferred_element_type=jnp.float32)


def attend_kernel(parts, mine, valid_ref, perm_ref, packed_ref, mask_ref, *refs):
    kv_refs = refs[:parts]
    w_any, keep_ref, send_ref, w_ref, sem = refs[parts:]
    copy = pltpu.make_async_copy(w_any, w_ref, sem)
    copy.start()
    rows = packed_ref.shape[0]
    lanes = mine * DH
    scale = DH ** (-0.5) * LOG2E
    perm = perm_ref[...]
    q = jnp.dot(perm, packed_ref[:, :lanes], preferred_element_type=jnp.float32).astype(jnp.bfloat16)
    q = jnp.concatenate([q[:, a * DH : (a + 1) * DH] for a in range(mine)], axis=0)

    def scores(keys):
        return (
            lax.dot_general(q, keys, (((1,), (1,)), ((), ())), preferred_element_type=jnp.float32)
            * scale
        )

    mask = jnp.dot(perm, mask_ref[...], preferred_element_type=jnp.float32)
    linked = jnp.concatenate([mask] * mine, axis=0) > 0.5
    s = jnp.where(linked, scores(packed_ref[:, lanes : lanes + DH]), NEG)
    top = jnp.max(s, axis=-1, keepdims=True)
    out = weigh(jnp.exp2(s - top), packed_ref[:, lanes + DH :])
    for part in range(parts):
        kv = kv_refs[part]
        place = lax.broadcasted_iota(jnp.int32, (1, kv.shape[0]), 1)
        bias = jnp.where(place < valid_ref[part], 0.0, NEG)
        s = scores(kv[:, :DH]) + bias
        peak = jnp.maximum(top, jnp.max(s, axis=-1, keepdims=True))
        out = out * jnp.exp2(top - peak) + weigh(jnp.exp2(s - peak), kv[:, DH:])
        top = peak
    attention = (out[:, :DH] / out[:, DH:]).astype(jnp.bfloat16)
    attention = jnp.concatenate(
        [attention[a * rows : (a + 1) * rows] for a in range(mine)], axis=1
    )
    copy.wait()
    half = rows // 2
    width = w_ref.shape[1]
    tile = min(width, 1024)
    for first in range(0, width, tile):
        piece = jnp.dot(
            attention, w_ref[:, first : first + tile], preferred_element_type=jnp.float32
        ).astype(jnp.bfloat16)
        keep_ref[:, first : first + tile] = piece[:half]
        send_ref[:, first : first + tile] = piece[half:]


def attend(valid, perm, packed, mask, blocks, w):
    parts = len(blocks)
    rows, mine = packed.shape[0], (packed.shape[1] - 2 * DH) // DH
    span = blocks[0].shape[0]
    full = pl.BlockSpec(memory_space=pltpu.VMEM)
    out = jax.ShapeDtypeStruct((rows // 2, w.shape[1]), jnp.bfloat16)
    reach = rows + parts * span
    return pl.pallas_call(
        functools.partial(attend_kernel, parts, mine),
        out_shape=(out, out),
        in_specs=[pl.BlockSpec(memory_space=pltpu.SMEM)]
        + [full] * (parts + 3)
        + [pl.BlockSpec(memory_space=pltpu.HBM)],
        out_specs=(full, full),
        scratch_shapes=[pltpu.VMEM(w.shape, w.dtype), pltpu.SemaphoreType.DMA],
        compiler_params=pltpu.CompilerParams(vmem_limit_bytes=ATTEND_LIMIT),
        cost_estimate=pl.CostEstimate(
            flops=4 * rows * mine * DH * reach + 2 * rows * mine * DH * w.shape[1],
            bytes_accessed=2 * w.size + 4 * DH * reach + 2 * rows * w.shape[1],
            transcendentals=rows * mine * reach,
        ),
    )(valid, perm, packed, mask, *blocks, w)


def seat_rows(first_ref, topk, table, back_ref, experts, seats):
    count = table.shape[0]
    block = min(count, 256)
    lane = lax.broadcasted_iota(jnp.int32, (count, DH), 1)
    hits = []
    spread = jnp.zeros((count, DH), jnp.float32)
    for e in range(experts):
        named = (first_ref[0] + e).astype(jnp.float32)
        match = jnp.where((table == named) & (lane < topk), 1.0, 0.0)
        hits.append(jnp.max(match, axis=1, keepdims=True))
        spread = spread + jnp.where(lane == e, hits[e], 0.0)
    ahead = lax.broadcasted_iota(jnp.int32, (block, block), 0) > lax.broadcasted_iota(
        jnp.int32, (block, block), 1
    )
    ahead = jnp.where(ahead, 1.0, 0.0).astype(jnp.bfloat16)
    place = lax.broadcasted_iota(jnp.int32, (block, seats), 1).astype(jnp.float32)
    carry = jnp.zeros((1, DH), jnp.float32)
    for at in range(0, count, block):
        here = spread[at : at + block]
        before = carry + jnp.dot(
            ahead, here.astype(jnp.bfloat16), preferred_element_type=jnp.float32
        )
        carry = carry + jnp.sum(here, axis=0, keepdims=True)
        for e in range(experts):
            seat = jnp.sum(jnp.where(lane[:block] == e, before, 0.0), axis=1, keepdims=True)
            taken = (hits[e][at : at + block] > 0.5) & (seat == place)
            back_ref[at : at + block, e * seats : (e + 1) * seats] = jnp.where(
                taken, 1.0, 0.0
            ).astype(jnp.bfloat16)


def pick_rows(back_ref, rows, first, width):
    return lax.dot_general(
        back_ref[...],
        rows[:, first : first + width],
        (((0,), (0,)), ((), ())),
        preferred_element_type=jnp.float32,
    )


def expert_kernel(pieces, experts, seats, topk, chunk, *refs):
    refs = list(refs)

    def take(count):
        out = refs[:count]
        del refs[:count]
        return out

    part_refs = take(pieces)
    wg_any, wu_any = take(2)
    if chunk == 0:
        first_ref, wd_any = take(2)
        gate_ref, up_ref, back_ref, rate_ref, ready_ref = take(5)
    else:
        gate_in, up_in, back_ref, rate_ref, ready_ref, wd_any = take(6)
        outs = take(3)
        hidden = outs[2]
    rows, picked, wg, wu, part_sem, gate_sem, up_sem = take(7)
    held, cut, wide = wg.shape
    per_expert = held // experts
    size = rows.shape[0] // pieces
    moves = [
        pltpu.make_async_copy(ref, rows.at[pl.ds(i * size, size)], part_sem.at[i])
        for i, ref in enumerate(part_refs)
    ]
    for move in moves:
        move.start()
    first = chunk * cut

    def weight_moves(p):
        return (
            pltpu.make_async_copy(wg_any.at[p, pl.ds(first, cut)], wg.at[p], gate_sem.at[p]),
            pltpu.make_async_copy(wu_any.at[p, pl.ds(first, cut)], wu.at[p], up_sem.at[p]),
        )

    for p in range(held):
        for move in weight_moves(p):
            move.start()
    if chunk == 0:
        (ready_sem,) = take(1)
        early = [
            pltpu.make_async_copy(wd_any.at[p], ready_ref.at[p], ready_sem.at[p])
            for p in range(ready_ref.shape[0])
        ]
        for move in early:
            move.start()
    else:
        wd, flat, down_sem = take(3)

        ready = ready_ref.shape[0]

        def down_move(p):
            place = pl.ds((p - ready) * wide, wide)
            return pltpu.make_async_copy(
                wd_any.at[p, :, pl.ds(0, cut)], wd.at[place], down_sem.at[p - ready]
            )

        for p in range(ready, held):
            down_move(p).start()
    for move in moves:
        move.wait()
    if chunk == 0:
        seat_rows(first_ref, topk, rows[:, cut:].astype(jnp.float32), back_ref, experts, seats)
        meta = pick_rows(back_ref, rows, cut, DH)
        lane = lax.broadcasted_iota(jnp.int32, (seats, DH), 1)
        for e in range(experts):
            named = (first_ref[0] + e).astype(jnp.float32)
            own = meta[e * seats : (e + 1) * seats]
            gates = pltpu.roll(own, DH - topk, 1)
            rate_ref[e] = jnp.sum(
                jnp.where((own == named) & (lane < topk), gates, 0.0), axis=1, keepdims=True
            )
    tile = 512 if cut % 512 == 0 else cut
    for c in range(0, cut, tile):
        picked[:, c : c + tile] = pick_rows(back_ref, rows, c, tile).astype(jnp.bfloat16)
    for e in range(experts):

        def panel(k, carry, e=e):
            p = e * per_expert + k
            for move in weight_moves(p):
                move.wait()
            w = jnp.concatenate([wg[p], wu[p]], axis=1)
            both = jnp.dot(
                picked[e * seats : (e + 1) * seats], w, preferred_element_type=jnp.float32
            )
            gate, up = both[:, :wide], both[:, wide:]
            if chunk:
                gate, up = gate + gate_in[p], up + up_in[p]
                value = gate / (1.0 + jnp.exp(-gate)) * up * rate_ref[e]
                place = pl.ds(pl.multiple_of(k * wide, wide), wide)
                hidden[e * seats : (e + 1) * seats, place] = value.astype(jnp.bfloat16)
            else:
                gate_ref[p] = gate
                up_ref[p] = up
            return carry

        lax.fori_loop(0, per_expert, panel, 0)
    if chunk == 0:
        for move in early:
            move.wait()
        return
    moves = [down_move(p) for p in range(ready, held)]
    drop_columns(hidden, ready_ref, wd, back_ref, flat, *outs[:2], moves)


def drop_columns(hidden, ready_ref, wd, back_ref, flat, keep_ref, send_ref, moves, first=0):
    cut = flat.shape[1]
    lines = hidden.shape[0]
    ready, wide, _ = ready_ref.shape
    per_expert = hidden.shape[1] // wide
    rest = 0 if wd is None else wd.shape[0] // wide
    experts = (ready + rest) // per_expert
    seats = lines // experts
    tile = 512 if cut % 512 == 0 else cut
    for e in range(experts):
        low, high = e * per_expert, (e + 1) * per_expert
        split = min(max(ready, low), high)
        for move in moves[split - ready : high - ready] if split < high else []:
            move.wait()
        for c in range(0, cut, tile):
            total = None
            if split > low:
                total = jnp.dot(
                    hidden[e * seats : (e + 1) * seats, : (split - low) * wide],
                    ready_ref[low:split, :, first + c : first + c + tile].reshape(-1, tile),
                    preferred_element_type=jnp.float32,
                )
            if split < high:
                rest = jnp.dot(
                    hidden[e * seats : (e + 1) * seats, (split - low) * wide :],
                    wd[(split - ready) * wide : (high - ready) * wide, c : c + tile],
                    preferred_element_type=jnp.float32,
                )
                total = rest if total is None else total + rest
            flat[e * seats : (e + 1) * seats, c : c + tile] = total.astype(jnp.bfloat16)
    half = keep_ref.shape[0]
    for c in range(0, cut, tile):
        moved = jnp.dot(
            back_ref[...], flat[:, c : c + tile], preferred_element_type=jnp.float32
        ).astype(jnp.bfloat16)
        keep_ref[:, c : c + tile] = moved[:half]
        send_ref[:, c : c + tile] = moved[half:]


def fall_kernel(hidden_ref, ready_ref, back_ref, wd_any, keep_ref, send_ref, flat, *refs):
    ready, wide, depth = ready_ref.shape
    cut = flat.shape[1]
    wd, moves = None, []
    if refs:
        wd, sem = refs
        moves = [
            pltpu.make_async_copy(
                wd_any.at[p, :, pl.ds(cut, cut)], wd.at[pl.ds((p - ready) * wide, wide)], sem.at[p - ready]
            )
            for p in range(ready, wd_any.shape[0])
        ]
        for move in moves:
            move.start()
    drop_columns(hidden_ref, ready_ref, wd, back_ref, flat, keep_ref, send_ref, moves, first=cut)


def fall_call(hidden, ready, back, w_down):
    held, wide, depth = w_down.shape
    rest = held - ready.shape[0]
    cut = depth // 2
    full = pl.BlockSpec(memory_space=pltpu.VMEM)
    shape = jax.ShapeDtypeStruct((back.shape[0] // 2, cut), jnp.bfloat16)
    scratch = [pltpu.VMEM((hidden.shape[0], cut), jnp.bfloat16)]
    if rest:
        scratch += [pltpu.VMEM((rest * wide, cut), jnp.bfloat16), pltpu.SemaphoreType.DMA((rest,))]
    return pl.pallas_call(
        fall_kernel,
        out_shape=(shape, shape),
        in_specs=[full, full, full, pl.BlockSpec(memory_space=pltpu.HBM)],
        out_specs=(full, full),
        scratch_shapes=scratch,
        compiler_params=pltpu.CompilerParams(vmem_limit_bytes=LAST_LIMIT),
        cost_estimate=pl.CostEstimate(
            flops=2 * held * hidden.shape[0] * cut * wide + 2 * hidden.shape[0] * back.shape[0] * cut,
            bytes_accessed=2 * rest * cut * wide,
            transcendentals=0,
        ),
    )(hidden, ready, back, w_down)


def expert_call(rows, w_gate, w_up, chunk, cut, topk, experts, seats, first=None, sums=None, w_down=None):
    held, depth, wide = w_gate.shape
    count = rows[0].shape[0] * len(rows)
    full = pl.BlockSpec(memory_space=pltpu.VMEM)
    anywhere = pl.BlockSpec(memory_space=pl.ANY)
    far = pl.BlockSpec(memory_space=pltpu.HBM)
    deep = held // experts * wide
    args = [*rows, w_gate, w_up]
    in_specs = [anywhere] * len(rows) + [far, far]
    scratch = [
        pltpu.VMEM((count, rows[0].shape[1]), jnp.bfloat16),
        pltpu.VMEM((experts * seats, cut), jnp.bfloat16),
        pltpu.VMEM((held, cut, wide), jnp.bfloat16),
        pltpu.VMEM((held, cut, wide), jnp.bfloat16),
        pltpu.SemaphoreType.DMA((len(rows),)),
        pltpu.SemaphoreType.DMA((held,)),
        pltpu.SemaphoreType.DMA((held,)),
    ]
    flops = 4 * held * seats * cut * wide + 2 * experts * seats * count * cut
    moved = 4 * held * cut * wide + 2 * count * cut
    if chunk == 0:
        early = max(1, held * READY // 16)
        args += [first, w_down]
        in_specs += [pl.BlockSpec(memory_space=pltpu.SMEM), far]
        outs = [jax.ShapeDtypeStruct((held, seats, wide), jnp.float32)] * 2 + [
            jax.ShapeDtypeStruct((count, experts * seats), jnp.bfloat16),
            jax.ShapeDtypeStruct((experts, seats, 1), jnp.float32),
            jax.ShapeDtypeStruct((early, wide, depth), jnp.bfloat16),
        ]
        scratch += [pltpu.SemaphoreType.DMA((early,))]
        moved += 2 * early * wide * depth
    else:
        ready = sums[4]
        args += [*sums, w_down]
        in_specs += [full] * 5 + [far]
        outs = [jax.ShapeDtypeStruct((count // 2, cut), jnp.bfloat16)] * 2
        outs += [jax.ShapeDtypeStruct((experts * seats, deep), jnp.bfloat16)]
        scratch += [
            pltpu.VMEM(((held - ready.shape[0]) * wide or 8, cut), jnp.bfloat16),
            pltpu.VMEM((experts * seats, cut), jnp.bfloat16),
            pltpu.SemaphoreType.DMA((max(1, held - ready.shape[0]),)),
        ]
        flops += 2 * held * seats * cut * wide + 2 * experts * seats * count * cut
        moved += held * depth * wide
    return pl.pallas_call(
        functools.partial(expert_kernel, len(rows), experts, seats, topk, chunk),
        out_shape=tuple(outs),
        in_specs=in_specs,
        out_specs=tuple([full] * len(outs)),
        scratch_shapes=scratch,
        compiler_params=pltpu.CompilerParams(vmem_limit_bytes=RISE_LIMIT if chunk == 0 else FALL_LIMIT),
        cost_estimate=pl.CostEstimate(
            flops=flops, bytes_accessed=moved, transcendentals=0
        ),
    )(*args)


def body(
    queries,
    kv_cache,
    tree_kv,
    context_lengths,
    tree_parents,
    resid,
    out_weight,
    norm_gain,
    expert_ids,
    gate_weights,
    w_gate,
    w_up,
    w_down,
):
    here = lax.axis_index("seq")
    there = lax.axis_index("req")
    parts = lax.axis_size("seq")
    groups = lax.axis_size("req")
    bits = parts.bit_length() - 1
    order = block_order(parts)
    near = order[: parts // 2]
    own = queries.shape[1]
    rows = own * parts
    depth = resid.shape[2]

    span = kv_cache.shape[1]
    share = parts // KVH
    lane = kv_cache[0]
    heads = [
        lane[:, :, h * DH : (h + 1) * DH].reshape(span, 2 * DH) for h in range(KVH)
    ]

    def head_of(device):
        pick = heads[0]
        for h in range(1, KVH):
            pick = jnp.where(device // share == h, heads[h], pick)
        return pick

    same, other = head_of(here), head_of(here ^ (parts // 2))
    turns = [near[0]] + ([near[i] for i in (2, 3, 1)] if len(near) == 4 else near[1:])
    order_kv = turns + [mask ^ 1 for mask in turns]
    half = [same] + [hop(other if mask & (parts // 2) else same, mask) for mask in turns[1:]]
    valid = context_lengths[0] - jnp.stack([(here ^ mask) * span for mask in order_kv])

    mine = HQ // parts
    tree_heads = [
        tree_kv[0][:, :, h * DH : (h + 1) * DH].reshape(own, 2 * DH) for h in range(KVH)
    ]
    asked = jnp.transpose(queries[0].reshape(own, parts, mine * DH), (1, 0, 2))
    trees = jnp.stack(tree_heads)[:, None]
    trees = jnp.broadcast_to(trees, (KVH, share, own, 2 * DH)).reshape(parts, own, 2 * DH)
    packed = jnp.concatenate([asked, trees], axis=2)
    packed = lax.all_to_all(packed, "seq", split_axis=0, concat_axis=0, tiled=True)
    packed = packed.reshape(rows, -1)

    wanted = jnp.stack([here ^ mask for mask in order])
    wanted = (wanted[:, None] * own + jnp.arange(own, dtype=jnp.int32)[None, :]).reshape(rows)
    perm = (wanted[:, None] == jnp.arange(rows, dtype=jnp.int32)[None, :]).astype(jnp.bfloat16)

    linked = ancestry(tree_parents[0])
    blocks = half + [hop(piece, 1) for piece in half]
    keep, send = attend(valid.astype(jnp.int32), perm, packed, linked, blocks, out_weight)

    got = hop(send, 1)
    pair = [
        keep[i * own : (i + 1) * own].astype(jnp.float32)
        + got[i * own : (i + 1) * own].astype(jnp.float32)
        for i in range(len(near))
    ]
    terms = [pair[0]] + [
        hop(pair[i].astype(jnp.bfloat16), near[i]).astype(jnp.float32)
        for i in range(1, len(near))
    ]
    attended = sum(terms[1:], terms[0]).astype(jnp.bfloat16)
    mid = (resid[0].astype(jnp.float32) + attended.astype(jnp.float32)).astype(jnp.bfloat16)
    midf = lax.optimization_barrier(mid).astype(jnp.float32)
    factor = lax.rsqrt(jnp.mean(midf * midf, axis=-1, keepdims=True) + EPS)
    normed = (midf * factor * norm_gain.astype(jnp.float32)).astype(jnp.bfloat16)

    table = jnp.concatenate(
        [expert_ids[0].astype(jnp.bfloat16), gate_weights[0]], axis=1
    )
    table = lax.dynamic_slice_in_dim(table, here * own, own, 0)
    topk = expert_ids.shape[2]
    table = jnp.pad(table, ((0, 0), (0, DH - 2 * topk)))
    held = w_gate.shape[0]
    experts = max(1, held // SPLIT)
    first = (((there * parts + here) * held) // SPLIT).astype(jnp.int32).reshape(1)
    seats = groups * CAP

    cut = depth // 2
    ring = [near[0]] + ([near[i] for i in (3, 1, 2)] if len(near) == 4 else near[1:])
    spin = [0] + ([1, 2, 3] if groups == 4 else list(range(1, groups)))
    planes = []
    for chunk in range(2):
        piece = normed[:, chunk * cut : (chunk + 1) * cut]
        if chunk == 0:
            piece = jnp.concatenate([piece, table], axis=1)
        stack = jnp.concatenate([piece] + [turn(piece, d) for d in spin[1:]], axis=0)
        planes.append([stack] + [hop(stack, mask) for mask in ring[1:]])
    full = planes[0] + [hop(p, 1) for p in planes[0]]
    sums = expert_call(full, w_gate, w_up, 0, cut, topk, experts, seats, first=first, w_down=w_down)
    plane = planes[1][:1]
    gate = sums[0]
    for piece in planes[1][1:]:
        plane.append(lax.optimization_barrier((piece, gate))[0])
    full = plane + [hop(p, 1) for p in plane]
    keep0, send0, hidden = expert_call(
        full, w_gate, w_up, 1, cut, topk, experts, seats, sums=(gate, *sums[1:]), w_down=w_down
    )

    size = groups * own

    def paired(keep, got):
        return {
            mask: keep[i * size : (i + 1) * size].astype(jnp.float32)
            + got[i * size : (i + 1) * size].astype(jnp.float32)
            for i, mask in enumerate(ring)
        }

    def send(value, mask):
        return hop(value.astype(jnp.bfloat16), mask).astype(jnp.float32)

    def home(flat):
        result = flat[:own]
        for i in range(groups - 1, 0, -1):
            result = result + turn(
                flat[i * own : (i + 1) * own].astype(jnp.bfloat16), spin[i]
            ).astype(jnp.float32)
        return result.astype(jnp.bfloat16)

    got0 = hop(send0, 1)
    keep1, send1 = fall_call(hidden, sums[4], sums[2], w_down)
    send1, got0 = lax.optimization_barrier((send1, got0))
    got1 = hop(send1, 1)
    low, high = paired(keep0, got0), paired(keep1, got1)
    if len(near) == 4:
        near_x, near_y = 2, 4
        far = near_x ^ near_y
        got_low, got_high = send(low[far], near_x), send(high[far], near_y)
        go_x, go_y = low[near_x].astype(jnp.bfloat16), (low[near_y] + got_low).astype(jnp.bfloat16)
        go_x, go_y, got_high = lax.optimization_barrier((go_x, go_y, got_high))
        got_x, got_y = send(go_x, near_x), send(go_y, near_y)
        flat_low = low[0] + got_x + got_y
        go_x, go_y = (high[near_x] + got_high).astype(jnp.bfloat16), high[near_y].astype(jnp.bfloat16)
        go_x, go_y, flat_low = lax.optimization_barrier((go_x, go_y, flat_low))
        flat_high = high[0] + send(go_x, near_x) + send(go_y, near_y)
    else:
        flat_low, flat_high = (
            sum([send(blocks[mask], mask) for mask in near[1:]], blocks[0]) for blocks in (low, high)
        )
    pieces = [home(flat_low), home(flat_high)]
    return (attended[None], jnp.concatenate(pieces, axis=1)[None])


def solution(mesh):
    placed = (
        P("req", "seq", None),
        P("req", "seq", None, None),
        P("req", "seq", None, None),
        P("req"),
        P("req", None),
        P("req", "seq", None),
        P("seq", None),
        P(),
        P("req", None, None),
        P("req", None, None),
        P(("req", "seq"), None, None),
        P(("req", "seq"), None, None),
        P(("req", "seq"), None, None),
    )
    return jax.shard_map(
        body,
        mesh=mesh,
        in_specs=placed,
        out_specs=(P("req", "seq", None), P("req", "seq", None)),
        check_vma=False,
    )
```

```python
import functools

import jax
import jax.numpy as jnp
from jax import lax
from jax.experimental import pallas as pl
from jax.experimental.pallas import tpu as pltpu
from jax.sharding import PartitionSpec as P

DH = 128
HQ = 32
KVH = 2
EXPERTS = 64
CAP = 32
SPLIT = 8


NEG = -1e30
EPS = 1e-06
RISE_LIMIT = 30 * 1024 * 1024
FALL_LIMIT = 29 * 1024 * 1024
LAST_LIMIT = 26 * 1024 * 1024
ATTEND_LIMIT = 48 * 1024 * 1024
READY = 12
LOG2E = 1.4426950408889634


def hop(value, mask):
    count = lax.axis_size("seq")
    return lax.ppermute(value, "seq", [(i, i ^ mask) for i in range(count)])


def turn(value, step):
    count = lax.axis_size("req")
    return lax.ppermute(value, "req", [(i, i ^ step) for i in range(count)])


def block_order(parts):
    bits = parts.bit_length() - 1
    return [int(format(p, "b").zfill(bits)[::-1], 2) if bits else 0 for p in range(parts)]


def ancestry(parents):
    count = parents.shape[0]
    node = jnp.arange(count, dtype=jnp.int32)
    linked = (parents[:, None] == node[None, :]) | (node[:, None] == node[None, :])
    reach = linked.astype(jnp.bfloat16)
    hops = 1
    while hops < count:
        paths = jnp.dot(reach, reach, preferred_element_type=jnp.float32)
        reach = jnp.minimum(paths, 1.0).astype(jnp.bfloat16)
        hops = hops * 2
    return reach


def weigh(weights, values):
    values = jnp.concatenate([values, jnp.ones_like(values)], axis=1)
    return jnp.dot(weights.astype(jnp.bfloat16), values, preferred_element_type=jnp.float32)


def attend_kernel(parts, mine, valid_ref, perm_ref, packed_ref, mask_ref, *refs):
    kv_refs = refs[:parts]
    w_any, keep_ref, send_ref, w_ref, sem = refs[parts:]
    copy = pltpu.make_async_copy(w_any, w_ref, sem)
    copy.start()
    rows = packed_ref.shape[0]
    lanes = mine * DH
    scale = DH ** (-0.5) * LOG2E
    perm = perm_ref[...]
    q = jnp.dot(perm, packed_ref[:, :lanes], preferred_element_type=jnp.float32).astype(jnp.bfloat16)
    q = jnp.concatenate([q[:, a * DH : (a + 1) * DH] for a in range(mine)], axis=0)

    def scores(keys):
        return (
            lax.dot_general(q, keys, (((1,), (1,)), ((), ())), preferred_element_type=jnp.float32)
            * scale
        )

    mask = jnp.dot(perm, mask_ref[...], preferred_element_type=jnp.float32)
    linked = jnp.concatenate([mask] * mine, axis=0) > 0.5
    s = jnp.where(linked, scores(packed_ref[:, lanes : lanes + DH]), NEG)
    top = jnp.max(s, axis=-1, keepdims=True)
    out = weigh(jnp.exp2(s - top), packed_ref[:, lanes + DH :])
    for part in range(parts):
        kv = kv_refs[part]
        place = lax.broadcasted_iota(jnp.int32, (1, kv.shape[0]), 1)
        bias = jnp.where(place < valid_ref[part], 0.0, NEG)
        s = scores(kv[:, :DH]) + bias
        peak = jnp.maximum(top, jnp.max(s, axis=-1, keepdims=True))
        out = out * jnp.exp2(top - peak) + weigh(jnp.exp2(s - peak), kv[:, DH:])
        top = peak
    attention = (out[:, :DH] / out[:, DH:]).astype(jnp.bfloat16)
    attention = jnp.concatenate(
        [attention[a * rows : (a + 1) * rows] for a in range(mine)], axis=1
    )
    copy.wait()
    half = rows // 2
    width = w_ref.shape[1]
    tile = min(width, 1024)
    for first in range(0, width, tile):
        piece = jnp.dot(
            attention, w_ref[:, first : first + tile], preferred_element_type=jnp.float32
        ).astype(jnp.bfloat16)
        keep_ref[:, first : first + tile] = piece[:half]
        send_ref[:, first : first + tile] = piece[half:]


def attend(valid, perm, packed, mask, blocks, w):
    parts = len(blocks)
    rows, mine = packed.shape[0], (packed.shape[1] - 2 * DH) // DH
    span = blocks[0].shape[0]
    full = pl.BlockSpec(memory_space=pltpu.VMEM)
    out = jax.ShapeDtypeStruct((rows // 2, w.shape[1]), jnp.bfloat16)
    reach = rows + parts * span
    return pl.pallas_call(
        functools.partial(attend_kernel, parts, mine),
        out_shape=(out, out),
        in_specs=[pl.BlockSpec(memory_space=pltpu.SMEM)]
        + [full] * (parts + 3)
        + [pl.BlockSpec(memory_space=pltpu.HBM)],
        out_specs=(full, full),
        scratch_shapes=[pltpu.VMEM(w.shape, w.dtype), pltpu.SemaphoreType.DMA],
        compiler_params=pltpu.CompilerParams(vmem_limit_bytes=ATTEND_LIMIT),
        cost_estimate=pl.CostEstimate(
            flops=4 * rows * mine * DH * reach + 2 * rows * mine * DH * w.shape[1],
            bytes_accessed=2 * w.size + 4 * DH * reach + 2 * rows * w.shape[1],
            transcendentals=rows * mine * reach,
        ),
    )(valid, perm, packed, mask, *blocks, w)


def seat_rows(first_ref, topk, table, back_ref, experts, seats):
    count = table.shape[0]
    block = min(count, 256)
    lane = lax.broadcasted_iota(jnp.int32, (count, DH), 1)
    hits = []
    spread = jnp.zeros((count, DH), jnp.float32)
    for e in range(experts):
        named = (first_ref[0] + e).astype(jnp.float32)
        match = jnp.where((table == named) & (lane < topk), 1.0, 0.0)
        hits.append(jnp.max(match, axis=1, keepdims=True))
        spread = spread + jnp.where(lane == e, hits[e], 0.0)
    ahead = lax.broadcasted_iota(jnp.int32, (block, block), 0) > lax.broadcasted_iota(
        jnp.int32, (block, block), 1
    )
    ahead = jnp.where(ahead, 1.0, 0.0).astype(jnp.bfloat16)
    place = lax.broadcasted_iota(jnp.int32, (block, seats), 1).astype(jnp.float32)
    carry = jnp.zeros((1, DH), jnp.float32)
    for at in range(0, count, block):
        here = spread[at : at + block]
        before = carry + jnp.dot(
            ahead, here.astype(jnp.bfloat16), preferred_element_type=jnp.float32
        )
        carry = carry + jnp.sum(here, axis=0, keepdims=True)
        for e in range(experts):
            seat = jnp.sum(jnp.where(lane[:block] == e, before, 0.0), axis=1, keepdims=True)
            taken = (hits[e][at : at + block] > 0.5) & (seat == place)
            back_ref[at : at + block, e * seats : (e + 1) * seats] = jnp.where(
                taken, 1.0, 0.0
            ).astype(jnp.bfloat16)


def pick_rows(back_ref, rows, first, width):
    return lax.dot_general(
        back_ref[...],
        rows[:, first : first + width],
        (((0,), (0,)), ((), ())),
        preferred_element_type=jnp.float32,
    )


def expert_kernel(pieces, experts, seats, topk, chunk, *refs):
    refs = list(refs)

    def take(count):
        out = refs[:count]
        del refs[:count]
        return out

    part_refs = take(pieces)
    wg_any, wu_any = take(2)
    if chunk == 0:
        first_ref, wd_any = take(2)
        gate_ref, up_ref, back_ref, rate_ref, ready_ref = take(5)
    else:
        gate_in, up_in, back_ref, rate_ref, ready_ref, wd_any = take(6)
        outs = take(3)
        hidden = outs[2]
    rows, picked, wg, wu, part_sem, gate_sem, up_sem = take(7)
    held, cut, wide = wg.shape
    per_expert = held // experts
    size = rows.shape[0] // pieces
    moves = [
        pltpu.make_async_copy(ref, rows.at[pl.ds(i * size, size)], part_sem.at[i])
        for i, ref in enumerate(part_refs)
    ]
    for move in moves:
        move.start()
    first = chunk * cut

    def weight_moves(p):
        return (
            pltpu.make_async_copy(wg_any.at[p, pl.ds(first, cut)], wg.at[p], gate_sem.at[p]),
            pltpu.make_async_copy(wu_any.at[p, pl.ds(first, cut)], wu.at[p], up_sem.at[p]),
        )

    for p in range(held):
        for move in weight_moves(p):
            move.start()
    if chunk == 0:
        (ready_sem,) = take(1)
        early = [
            pltpu.make_async_copy(wd_any.at[p], ready_ref.at[p], ready_sem.at[p])
            for p in range(ready_ref.shape[0])
        ]
        for move in early:
            move.start()
    else:
        wd, flat, down_sem = take(3)

        ready = ready_ref.shape[0]

        def down_move(p):
            place = pl.ds((p - ready) * wide, wide)
            return pltpu.make_async_copy(
                wd_any.at[p, :, pl.ds(0, cut)], wd.at[place], down_sem.at[p - ready]
            )

        for p in range(ready, held):
            down_move(p).start()
    for move in moves:
        move.wait()
    if chunk == 0:
        seat_rows(first_ref, topk, rows[:, cut:].astype(jnp.float32), back_ref, experts, seats)
        meta = pick_rows(back_ref, rows, cut, DH)
        lane = lax.broadcasted_iota(jnp.int32, (seats, DH), 1)
        for e in range(experts):
            named = (first_ref[0] + e).astype(jnp.float32)
            own = meta[e * seats : (e + 1) * seats]
            gates = pltpu.roll(own, DH - topk, 1)
            rate_ref[e] = jnp.sum(
                jnp.where((own == named) & (lane < topk), gates, 0.0), axis=1, keepdims=True
            )
    tile = 512 if cut % 512 == 0 else cut
    for c in range(0, cut, tile):
        picked[:, c : c + tile] = pick_rows(back_ref, rows, c, tile).astype(jnp.bfloat16)
    for e in range(experts):

        def panel(k, carry, e=e):
            p = e * per_expert + k
            for move in weight_moves(p):
                move.wait()
            w = jnp.concatenate([wg[p], wu[p]], axis=1)
            both = jnp.dot(
                picked[e * seats : (e + 1) * seats], w, preferred_element_type=jnp.float32
            )
            gate, up = both[:, :wide], both[:, wide:]
            if chunk:
                gate, up = gate + gate_in[p], up + up_in[p]
                value = gate / (1.0 + jnp.exp(-gate)) * up * rate_ref[e]
                place = pl.ds(pl.multiple_of(k * wide, wide), wide)
                hidden[e * seats : (e + 1) * seats, place] = value.astype(jnp.bfloat16)
            else:
                gate_ref[p] = gate
                up_ref[p] = up
            return carry

        lax.fori_loop(0, per_expert, panel, 0)
    if chunk == 0:
        for move in early:
            move.wait()
        return
    moves = [down_move(p) for p in range(ready, held)]
    drop_columns(hidden, ready_ref, wd, back_ref, flat, *outs[:2], moves)


def drop_columns(hidden, ready_ref, wd, back_ref, flat, keep_ref, send_ref, moves, first=0):
    cut = flat.shape[1]
    lines = hidden.shape[0]
    ready, wide, _ = ready_ref.shape
    per_expert = hidden.shape[1] // wide
    rest = 0 if wd is None else wd.shape[0] // wide
    experts = (ready + rest) // per_expert
    seats = lines // experts
    tile = 512 if cut % 512 == 0 else cut
    for e in range(experts):
        low, high = e * per_expert, (e + 1) * per_expert
        split = min(max(ready, low), high)
        for move in moves[split - ready : high - ready] if split < high else []:
            move.wait()
        for c in range(0, cut, tile):
            total = None
            if split > low:
                total = jnp.dot(
                    hidden[e * seats : (e + 1) * seats, : (split - low) * wide],
                    ready_ref[low:split, :, first + c : first + c + tile].reshape(-1, tile),
                    preferred_element_type=jnp.float32,
                )
            if split < high:
                rest = jnp.dot(
                    hidden[e * seats : (e + 1) * seats, (split - low) * wide :],
                    wd[(split - ready) * wide : (high - ready) * wide, c : c + tile],
                    preferred_element_type=jnp.float32,
                )
                total = rest if total is None else total + rest
            flat[e * seats : (e + 1) * seats, c : c + tile] = total.astype(jnp.bfloat16)
    half = keep_ref.shape[0]
    for c in range(0, cut, tile):
        moved = jnp.dot(
            back_ref[...], flat[:, c : c + tile], preferred_element_type=jnp.float32
        ).astype(jnp.bfloat16)
        keep_ref[:, c : c + tile] = moved[:half]
        send_ref[:, c : c + tile] = moved[half:]


def fall_kernel(hidden_ref, ready_ref, back_ref, wd_any, keep_ref, send_ref, flat, *refs):
    ready, wide, depth = ready_ref.shape
    cut = flat.shape[1]
    wd, moves = None, []
    if refs:
        wd, sem = refs
        moves = [
            pltpu.make_async_copy(
                wd_any.at[p, :, pl.ds(cut, cut)], wd.at[pl.ds((p - ready) * wide, wide)], sem.at[p - ready]
            )
            for p in range(ready, wd_any.shape[0])
        ]
        for move in moves:
            move.start()
    drop_columns(hidden_ref, ready_ref, wd, back_ref, flat, keep_ref, send_ref, moves, first=cut)


def fall_call(hidden, ready, back, w_down):
    held, wide, depth = w_down.shape
    rest = held - ready.shape[0]
    cut = depth // 2
    full = pl.BlockSpec(memory_space=pltpu.VMEM)
    shape = jax.ShapeDtypeStruct((back.shape[0] // 2, cut), jnp.bfloat16)
    scratch = [pltpu.VMEM((hidden.shape[0], cut), jnp.bfloat16)]
    if rest:
        scratch += [pltpu.VMEM((rest * wide, cut), jnp.bfloat16), pltpu.SemaphoreType.DMA((rest,))]
    return pl.pallas_call(
        fall_kernel,
        out_shape=(shape, shape),
        in_specs=[full, full, full, pl.BlockSpec(memory_space=pltpu.HBM)],
        out_specs=(full, full),
        scratch_shapes=scratch,
        compiler_params=pltpu.CompilerParams(vmem_limit_bytes=LAST_LIMIT),
        cost_estimate=pl.CostEstimate(
            flops=2 * held * hidden.shape[0] * cut * wide + 2 * hidden.shape[0] * back.shape[0] * cut,
            bytes_accessed=2 * rest * cut * wide,
            transcendentals=0,
        ),
    )(hidden, ready, back, w_down)


def expert_call(rows, w_gate, w_up, chunk, cut, topk, experts, seats, first=None, sums=None, w_down=None):
    held, depth, wide = w_gate.shape
    count = rows[0].shape[0] * len(rows)
    full = pl.BlockSpec(memory_space=pltpu.VMEM)
    anywhere = pl.BlockSpec(memory_space=pl.ANY)
    far = pl.BlockSpec(memory_space=pltpu.HBM)
    deep = held // experts * wide
    args = [*rows, w_gate, w_up]
    in_specs = [anywhere] * len(rows) + [far, far]
    scratch = [
        pltpu.VMEM((count, rows[0].shape[1]), jnp.bfloat16),
        pltpu.VMEM((experts * seats, cut), jnp.bfloat16),
        pltpu.VMEM((held, cut, wide), jnp.bfloat16),
        pltpu.VMEM((held, cut, wide), jnp.bfloat16),
        pltpu.SemaphoreType.DMA((len(rows),)),
        pltpu.SemaphoreType.DMA((held,)),
        pltpu.SemaphoreType.DMA((held,)),
    ]
    flops = 4 * held * seats * cut * wide + 2 * experts * seats * count * cut
    moved = 4 * held * cut * wide + 2 * count * cut
    if chunk == 0:
        early = max(1, held * READY // 16)
        args += [first, w_down]
        in_specs += [pl.BlockSpec(memory_space=pltpu.SMEM), far]
        outs = [jax.ShapeDtypeStruct((held, seats, wide), jnp.float32)] * 2 + [
            jax.ShapeDtypeStruct((count, experts * seats), jnp.bfloat16),
            jax.ShapeDtypeStruct((experts, seats, 1), jnp.float32),
            jax.ShapeDtypeStruct((early, wide, depth), jnp.bfloat16),
        ]
        scratch += [pltpu.SemaphoreType.DMA((early,))]
        moved += 2 * early * wide * depth
    else:
        ready = sums[4]
        args += [*sums, w_down]
        in_specs += [full] * 5 + [far]
        outs = [jax.ShapeDtypeStruct((count // 2, cut), jnp.bfloat16)] * 2
        outs += [jax.ShapeDtypeStruct((experts * seats, deep), jnp.bfloat16)]
        scratch += [
            pltpu.VMEM(((held - ready.shape[0]) * wide or 8, cut), jnp.bfloat16),
            pltpu.VMEM((experts * seats, cut), jnp.bfloat16),
            pltpu.SemaphoreType.DMA((max(1, held - ready.shape[0]),)),
        ]
        flops += 2 * held * seats * cut * wide + 2 * experts * seats * count * cut
        moved += held * depth * wide
    return pl.pallas_call(
        functools.partial(expert_kernel, len(rows), experts, seats, topk, chunk),
        out_shape=tuple(outs),
        in_specs=in_specs,
        out_specs=tuple([full] * len(outs)),
        scratch_shapes=scratch,
        compiler_params=pltpu.CompilerParams(vmem_limit_bytes=RISE_LIMIT if chunk == 0 else FALL_LIMIT),
        cost_estimate=pl.CostEstimate(
            flops=flops, bytes_accessed=moved, transcendentals=0
        ),
    )(*args)


def body(
    queries,
    kv_cache,
    tree_kv,
    context_lengths,
    tree_parents,
    resid,
    out_weight,
    norm_gain,
    expert_ids,
    gate_weights,
    w_gate,
    w_up,
    w_down,
):
    here = lax.axis_index("seq")
    there = lax.axis_index("req")
    parts = lax.axis_size("seq")
    groups = lax.axis_size("req")
    bits = parts.bit_length() - 1
    order = block_order(parts)
    near = order[: parts // 2]
    own = queries.shape[1]
    rows = own * parts
    depth = resid.shape[2]

    span = kv_cache.shape[1]
    share = parts // KVH
    lane = kv_cache[0]
    def head_of(device):
        first = (device // share) * DH
        return lax.dynamic_slice_in_dim(lane, first, DH, 2).reshape(span, 2 * DH)

    same, other = head_of(here), head_of(here ^ (parts // 2))
    turns = [near[0]] + ([near[i] for i in (2, 3, 1)] if len(near) == 4 else near[1:])
    order_kv = turns + [mask ^ 1 for mask in turns]
    half = [same] + [hop(other if mask & (parts // 2) else same, mask) for mask in turns[1:]]
    valid = context_lengths[0] - jnp.stack([(here ^ mask) * span for mask in order_kv])

    mine = HQ // parts
    tree_heads = [
        tree_kv[0][:, :, h * DH : (h + 1) * DH].reshape(own, 2 * DH) for h in range(KVH)
    ]
    asked = jnp.transpose(queries[0].reshape(own, parts, mine * DH), (1, 0, 2))
    trees = jnp.stack(tree_heads)[:, None]
    trees = jnp.broadcast_to(trees, (KVH, share, own, 2 * DH)).reshape(parts, own, 2 * DH)
    packed = jnp.concatenate([asked, trees], axis=2)
    packed = lax.all_to_all(packed, "seq", split_axis=0, concat_axis=0, tiled=True)
    packed = packed.reshape(rows, -1)

    wanted = jnp.stack([here ^ mask for mask in order])
    wanted = (wanted[:, None] * own + jnp.arange(own, dtype=jnp.int32)[None, :]).reshape(rows)
    perm = (wanted[:, None] == jnp.arange(rows, dtype=jnp.int32)[None, :]).astype(jnp.bfloat16)

    linked = ancestry(tree_parents[0])
    blocks = half + [hop(piece, 1) for piece in half]
    keep, send = attend(valid.astype(jnp.int32), perm, packed, linked, blocks, out_weight)

    got = hop(send, 1)
    pair = [
        keep[i * own : (i + 1) * own].astype(jnp.float32)
        + got[i * own : (i + 1) * own].astype(jnp.float32)
        for i in range(len(near))
    ]
    terms = [pair[0]] + [
        hop(pair[i].astype(jnp.bfloat16), near[i]).astype(jnp.float32)
        for i in range(1, len(near))
    ]
    attended = sum(terms[1:], terms[0]).astype(jnp.bfloat16)
    mid = (resid[0].astype(jnp.float32) + attended.astype(jnp.float32)).astype(jnp.bfloat16)
    midf = lax.optimization_barrier(mid).astype(jnp.float32)
    factor = lax.rsqrt(jnp.mean(midf * midf, axis=-1, keepdims=True) + EPS)
    normed = (midf * factor * norm_gain.astype(jnp.float32)).astype(jnp.bfloat16)

    table = jnp.concatenate(
        [expert_ids[0].astype(jnp.bfloat16), gate_weights[0]], axis=1
    )
    table = lax.dynamic_slice_in_dim(table, here * own, own, 0)
    topk = expert_ids.shape[2]
    table = jnp.pad(table, ((0, 0), (0, DH - 2 * topk)))
    held = w_gate.shape[0]
    experts = max(1, held // SPLIT)
    first = (((there * parts + here) * held) // SPLIT).astype(jnp.int32).reshape(1)
    seats = groups * CAP

    cut = depth // 2
    ring = [near[0]] + ([near[i] for i in (3, 1, 2)] if len(near) == 4 else near[1:])
    spin = [0] + ([1, 2, 3] if groups == 4 else list(range(1, groups)))
    planes = []
    for chunk in range(2):
        piece = normed[:, chunk * cut : (chunk + 1) * cut]
        if chunk == 0:
            piece = jnp.concatenate([piece, table], axis=1)
        stack = jnp.concatenate([piece] + [turn(piece, d) for d in spin[1:]], axis=0)
        planes.append([stack] + [hop(stack, mask) for mask in ring[1:]])
    full = planes[0] + [hop(p, 1) for p in planes[0]]
    sums = expert_call(full, w_gate, w_up, 0, cut, topk, experts, seats, first=first, w_down=w_down)
    plane = planes[1][:1]
    gate = sums[0]
    for piece in planes[1][1:]:
        plane.append(lax.optimization_barrier((piece, gate))[0])
    full = plane + [hop(p, 1) for p in plane]
    keep0, send0, hidden = expert_call(
        full, w_gate, w_up, 1, cut, topk, experts, seats, sums=(gate, *sums[1:]), w_down=w_down
    )

    size = groups * own

    def paired(keep, got):
        return {
            mask: keep[i * size : (i + 1) * size].astype(jnp.float32)
            + got[i * size : (i + 1) * size].astype(jnp.float32)
            for i, mask in enumerate(ring)
        }

    def send(value, mask):
        return hop(value.astype(jnp.bfloat16), mask).astype(jnp.float32)

    def home(flat):
        result = flat[:own]
        for i in range(groups - 1, 0, -1):
            result = result + turn(
                flat[i * own : (i + 1) * own].astype(jnp.bfloat16), spin[i]
            ).astype(jnp.float32)
        return result.astype(jnp.bfloat16)

    got0 = hop(send0, 1)
    keep1, send1 = fall_call(hidden, sums[4], sums[2], w_down)
    send1, got0 = lax.optimization_barrier((send1, got0))
    got1 = hop(send1, 1)
    low, high = paired(keep0, got0), paired(keep1, got1)
    if len(near) == 4:
        near_x, near_y = 2, 4
        far = near_x ^ near_y
        got_low, got_high = send(low[far], near_x), send(high[far], near_y)
        go_x, go_y = low[near_x].astype(jnp.bfloat16), (low[near_y] + got_low).astype(jnp.bfloat16)
        go_x, go_y, got_high = lax.optimization_barrier((go_x, go_y, got_high))
        got_x, got_y = send(go_x, near_x), send(go_y, near_y)
        flat_low = low[0] + got_x + got_y
        go_x, go_y = (high[near_x] + got_high).astype(jnp.bfloat16), high[near_y].astype(jnp.bfloat16)
        go_x, go_y, flat_low = lax.optimization_barrier((go_x, go_y, flat_low))
        flat_high = high[0] + send(go_x, near_x) + send(go_y, near_y)
    else:
        flat_low, flat_high = (
            sum([send(blocks[mask], mask) for mask in near[1:]], blocks[0]) for blocks in (low, high)
        )
    pieces = [home(flat_low), home(flat_high)]
    return (attended[None], jnp.concatenate(pieces, axis=1)[None])


def solution(mesh):
    placed = (
        P("req", "seq", None),
        P("req", "seq", None, None),
        P("req", "seq", None, None),
        P("req"),
        P("req", None),
        P("req", "seq", None),
        P("seq", None),
        P(),
        P("req", None, None),
        P("req", None, None),
        P(("req", "seq"), None, None),
        P(("req", "seq"), None, None),
        P(("req", "seq"), None, None),
    )
    return jax.shard_map(
        body,
        mesh=mesh,
        in_specs=placed,
        out_specs=(P("req", "seq", None), P("req", "seq", None)),
        check_vma=False,
    )
```
